32 devices in a mesh: gr: 4 (over y, core), gc: 8 (over z, x).
Axes of the slice: x: 2, y: 2, z: 4, core: 2. Of those that a mesh axis runs over, the one named last changes fastest.
Arguments:
- weights: bfloat16 [2048, 2048], P('gc', 'gr'), may hold values from 0.049804688 to 5
- in_pattern: int32 [16, 16], P('gc', 'gr'), may hold values from 0 to 1, as said below
- out_pattern: int32 [16, 16], P('gc', 'gr'), may hold values from 0 to 1, as said below
Outputs:
- next_matrix: bfloat16 [2048, 2048], P('gc', 'gr')
The draws below stay inside these ranges and needn't reach their ends.
Inputs may be any that keep to these rules, and one draw needn't show every extreme that they name: `in_pattern`: 0 or 1 a block; every diagonal block is 1; each aligned tile of 2 block rows by 4 block columns holds at most 4 ones, and one such tile holds exactly 4. `out_pattern`: 0 or 1 a block; every diagonal block is 1.
All inputs are finite; a program needn't handle non-finite values.
Results may differ from the reference program's by a relative error of at most 0.0055.
Values may be sent and summed in bfloat16 or wider, within the bound.
No kernel may reach another device: no remote copies, remote signals or barrier semaphores. Data moves between devices by JAX's collectives and lax.ppermute only.
A program may use at most 128 MiB of HBM per device.

```python
import math
import jax
import jax.numpy as jnp
from jax import lax

BLK = 128
BR_DEV = 2
BC_DEV = 4
CAP = 4
N = 2048
NB = 16


def draw_in_pattern(key, part):
    key_scores, key_counts, key_whole = jax.random.split(jax.random.fold_in(key, 11), 3)
    row_ids = jnp.arange(NB, dtype=jnp.int32)[:, None]
    col_ids = jnp.arange(NB, dtype=jnp.int32)[None, :]
    diagonal = row_ids == col_ids
    scores = jax.random.randint(key_scores, (NB, NB), 0, 1 << 20)
    scores = jnp.where(diagonal, -1, scores)
    tile_rows = NB // BR_DEV
    tile_cols = NB // BC_DEV
    within = BR_DEV * BC_DEV
    tiled_scores = scores.reshape(tile_rows, BR_DEV, tile_cols, BC_DEV).transpose(0, 2, 1, 3).reshape(tile_rows, tile_cols, within)
    forced = diagonal.astype(jnp.int32).reshape(tile_rows, BR_DEV, tile_cols, BC_DEV).sum(axis=(1, 3))
    ordinal = jnp.argsort(jnp.argsort(tiled_scores, axis=-1, stable=True), axis=-1, stable=True)
    counts = jax.random.randint(key_counts, (tile_rows, tile_cols), 0, CAP + 1)
    counts = jnp.maximum(counts, forced)
    whole_tile = jax.random.randint(key_whole, (), 0, tile_rows * tile_cols)
    tile_numbers = jnp.arange(tile_rows * tile_cols, dtype=jnp.int32).reshape(tile_rows, tile_cols)
    counts = jnp.where(tile_numbers == whole_tile, CAP, counts)
    block_flags = (ordinal < counts[:, :, None]).astype(jnp.int32)
    return block_flags.reshape(tile_rows, tile_cols, BR_DEV, BC_DEV).transpose(0, 2, 1, 3).reshape(NB, NB)


def draw_out_pattern(key, part):
    row_ids = jnp.arange(NB, dtype=jnp.int32)[:, None]
    col_ids = jnp.arange(NB, dtype=jnp.int32)[None, :]
    keeping = jax.random.randint(jax.random.fold_in(key, 23), (NB, NB), 0, 3) > 0
    return jnp.logical_or(keeping, row_ids == col_ids).astype(jnp.int32)


def block_scale(key, extent, cuts, smallest, top_value):
    loudness, own = 1.0, jax.random.fold_in(key, 6)
    for axis_at, shards_of in cuts:
        steps = jnp.exp(jax.random.uniform(jax.random.fold_in(own, axis_at), (shards_of,), jnp.float32, smallest / len(cuts), top_value / len(cuts)))
        loudness = loudness * jnp.repeat(steps, extent[axis_at] // shards_of).reshape([-1 if axis == axis_at else 1 for axis in range(len(extent))])
    return loudness


def setup_inputs(seed: int = 0) -> dict:
    streams_of = jax.random.split(jax.random.key(seed), 4)
    weights = jnp.clip(jnp.exp(math.log(5.0) - 4.609084 * jax.random.uniform(streams_of[0], (N, N), jnp.float32) ** block_scale(streams_of[0], (N, N), ((0, 8), (1, 4)), -0.2, 0.2)), 0.049804688, 5.0).astype(jnp.bfloat16)
    in_pattern = draw_in_pattern(jax.random.fold_in(streams_of[3], 71), 0)
    out_pattern = draw_out_pattern(jax.random.fold_in(streams_of[3], 71), 0)
    return {"weights": weights, "in_pattern": in_pattern, "out_pattern": out_pattern}


def expand_flags(block_flags):
    return jnp.repeat(jnp.repeat(block_flags, BLK, axis=0), BLK, axis=1)


def reference(weights, in_pattern, out_pattern):
    masked = weights * expand_flags(in_pattern).astype(jnp.bfloat16)
    input_total = jnp.sum(masked.astype(jnp.float32), axis=0)
    inverse = 1.0 / input_total
    stochastic = (masked.astype(jnp.float32) * inverse[None, :]).astype(jnp.bfloat16)
    wide_copy = stochastic.astype(jnp.float32)
    expanded = jnp.dot(wide_copy, wide_copy, precision=lax.Precision.HIGHEST, preferred_element_type=jnp.float32)
    pruned = expanded * expand_flags(out_pattern).astype(jnp.float32)
    inflated = pruned * pruned
    output_total = jnp.sum(inflated, axis=0)
    return ((inflated / output_total[None, :]) * float(N)).astype(jnp.bfloat16)
```

```python
import functools

import jax
import jax.numpy as jnp
from jax import lax
from jax.experimental import pallas as pl
from jax.experimental.pallas import tpu as pltpu
from jax.sharding import PartitionSpec as P

SLOTS = 4
META = 16
VMEM = pl.BlockSpec(memory_space=pltpu.VMEM)
SMEM = pl.BlockSpec(memory_space=pltpu.SMEM)


def bits_of(size):
    return [1 << b for b in reversed(range(size.bit_length() - 1))]


def swap(x, axis, bit):
    return lax.ppermute(x, axis, [(i, i ^ bit) for i in range(lax.axis_size(axis))])


def gather_xor(x, axis):
    held = {0: x}
    for bit in bits_of(lax.axis_size(axis)):
        held.update({m | bit: swap(v, axis, bit) for m, v in list(held.items())})
    return [held[m] for m in range(len(held))]


def total_over(x, axis):
    for bit in bits_of(lax.axis_size(axis)):
        x = x + swap(x, axis, bit)
    return x


def pack_kernel(flags_ref, weights_ref, packet_ref, sums_ref):
    blk_rows, blk_cols = flags_ref.shape
    size = weights_ref.shape[0] // blk_rows
    blocks = blk_rows * blk_cols
    flags = [flags_ref[b // blk_cols, b % blk_cols] for b in range(blocks)]
    count = sum(flags)
    ones, zeros, slots = 0, 0, []
    for b in range(blocks):
        slots.append(jnp.where(flags[b] == 1, ones, count + zeros))
        ones, zeros = ones + flags[b], zeros + (1 - flags[b])
    sums_ref[...] = jnp.zeros_like(sums_ref)
    row_ids = lax.broadcasted_iota(jnp.int32, (META, size), 0)
    meta = jnp.zeros((META, size), jnp.float32)
    for s in range(SLOTS):
        place = sum(jnp.where(slots[b] == s, b, 0) for b in range(blocks))
        row = pl.multiple_of(place // blk_cols * size, size)
        col = pl.multiple_of(place % blk_cols * size, size)
        block = weights_ref[pl.ds(row, size), pl.ds(col, size)]
        block = jnp.where(s < count, block, jnp.zeros_like(block))
        packet_ref[pl.ds(s * size, size), :] = block
        sums_ref[:, pl.ds(col, size)] += jnp.sum(block.astype(jnp.float32), axis=0, keepdims=True)
        meta = jnp.where(row_ids == s, place.astype(jnp.float32), meta)
    packet_ref[pl.ds(SLOTS * size, META), :] = meta.astype(packet_ref.dtype)


def expand_kernel(gr_size, gc_size, blk_rows, blk_cols, *refs):
    out_flags_ref, totals_ref = refs[:2]
    left_refs = refs[2 : 2 + gr_size]
    right_refs = refs[2 + gr_size : 2 + gr_size + gc_size]
    inflated_ref, sums_ref, left, right = refs[2 + gr_size + gc_size :]
    size = left.shape[0] // blk_rows
    my_col, my_row = lax.axis_index("gr"), lax.axis_index("gc")

    def places(ref):
        meta = ref[pl.ds(SLOTS * size, META), :].astype(jnp.float32)
        return [jnp.max(meta[s : s + 1, :]).astype(jnp.int32) for s in range(SLOTS)]

    inverse = 1.0 / totals_ref[...]
    left[...] = jnp.zeros_like(left)
    right[...] = jnp.zeros_like(right)
    for m, ref in enumerate(left_refs):
        base = (my_col ^ m) * blk_cols
        for s, place in enumerate(places(ref)):
            row = pl.multiple_of(place // blk_cols * size, size)
            col = place % blk_cols
            scale = inverse[m : m + 1, :size]
            for j in range(1, blk_cols):
                scale = jnp.where(col == j, inverse[m : m + 1, j * size : (j + 1) * size], scale)
            block = ref[pl.ds(s * size, size), :].astype(jnp.float32) * scale
            at = pl.multiple_of((base + col) * size, size)
            left[pl.ds(row, size), pl.ds(at, size)] = block.astype(left.dtype)
    for m, ref in enumerate(right_refs):
        base = (my_row ^ m) * blk_rows
        for s, place in enumerate(places(ref)):
            row = pl.multiple_of((base + place // blk_cols) * size, size)
            col = pl.multiple_of(place % blk_cols * size, size)
            right[pl.ds(row, size), pl.ds(col, size)] = ref[pl.ds(s * size, size), :]
    product = jnp.dot(left[...], right[...], preferred_element_type=jnp.float32)
    for j in range(blk_cols):
        at = slice(j * size, (j + 1) * size)
        total = jnp.zeros((1, size), jnp.float32)
        for i in range(blk_rows):
            rows = slice(i * size, (i + 1) * size)
            kept = product[rows, at] * inverse[0:1, at]
            kept = kept * out_flags_ref[i, j].astype(jnp.float32)
            squared = kept * kept
            inflated_ref[rows, at] = squared
            total = total + jnp.sum(squared, axis=0, keepdims=True)
        sums_ref[:, at] = total


def shards(weights, in_pattern, out_pattern):
    blk_rows, blk_cols = in_pattern.shape
    local_rows, local_cols = weights.shape
    size = local_rows // blk_rows
    gr_size, gc_size = lax.axis_size("gr"), lax.axis_size("gc")
    order_size = local_rows * gc_size
    packet, sums = pl.pallas_call(
        pack_kernel,
        out_shape=(
            jax.ShapeDtypeStruct((SLOTS * size + META, size), weights.dtype),
            jax.ShapeDtypeStruct((1, local_cols), jnp.float32),
        ),
        in_specs=[SMEM, VMEM],
        out_specs=(VMEM, VMEM),
        name="pack",
    )(in_pattern, weights)
    totals = total_over(jnp.concatenate(gather_xor(sums, "gr"), axis=0), "gc")
    left = gather_xor(packet, "gr")
    right = gather_xor(packet, "gc")
    inflated, sums = pl.pallas_call(
        functools.partial(expand_kernel, gr_size, gc_size, blk_rows, blk_cols),
        out_shape=(
            jax.ShapeDtypeStruct((local_rows, local_cols), jnp.float32),
            jax.ShapeDtypeStruct((1, local_cols), jnp.float32),
        ),
        in_specs=[SMEM, VMEM] + [VMEM] * (gr_size + gc_size),
        out_specs=(VMEM, VMEM),
        scratch_shapes=[
            pltpu.VMEM((local_rows, order_size), jnp.bfloat16),
            pltpu.VMEM((order_size, local_cols), jnp.bfloat16),
        ],
        compiler_params=pltpu.CompilerParams(vmem_limit_bytes=40 << 20),
        name="expand",
    )(out_pattern, totals, *left, *right)
    output_total = total_over(sums, "gc")
    return (inflated / output_total * float(order_size)).astype(jnp.bfloat16)


def solution(mesh):
    in_specs = (P("gc", "gr"), P("gc", "gr"), P("gc", "gr"))
    out_specs = P("gc", "gr")
    return jax.shard_map(shards, mesh=mesh, in_specs=in_specs, out_specs=out_specs, check_vma=False)
```

```python
import functools

import jax
import jax.numpy as jnp
from jax import lax
from jax.experimental import pallas as pl
from jax.experimental.pallas import tpu as pltpu
from jax.sharding import PartitionSpec as P

SLOTS = 4
META = 16
VMEM = pl.BlockSpec(memory_space=pltpu.VMEM)
SMEM = pl.BlockSpec(memory_space=pltpu.SMEM)


def bits_of(size):
    return [1 << b for b in reversed(range(size.bit_length() - 1))]


def swap(x, axis, bit):
    return lax.ppermute(x, axis, [(i, i ^ bit) for i in range(lax.axis_size(axis))])


def gather_xor(x, axis):
    held = {0: x}
    for m in sorted(range(1, lax.axis_size(axis)), key=lambda m: (m.bit_count(), -m)):
        bits = [bit for bit in bits_of(lax.axis_size(axis)) if m & bit]
        last = bits[min(1, len(bits) - 1)]
        held[m] = swap(held[m ^ last], axis, last)
    return [held[m] for m in range(len(held))]


def total_over(x, axis):
    for bit in bits_of(lax.axis_size(axis)):
        x = x + swap(x, axis, bit)
    return x


def total_at_once(x, axis):
    size = lax.axis_size(axis)
    parts = lax.all_to_all(jnp.broadcast_to(x[None], (size,) + x.shape), axis, 0, 0)
    return jnp.sum(parts, axis=0)


def places_in(packet_ref, size):
    meta = packet_ref[pl.ds(SLOTS * size, META), :].astype(jnp.float32)
    return [jnp.max(meta[s : s + 1, :]).astype(jnp.int32) for s in range(SLOTS)]


def pack_kernel(flags_ref, weights_ref, packet_ref):
    blk_rows, blk_cols = flags_ref.shape
    size = weights_ref.shape[0] // blk_rows
    blocks = blk_rows * blk_cols
    flags = [flags_ref[b // blk_cols, b % blk_cols] for b in range(blocks)]
    count = sum(flags)
    ones, zeros, slots = 0, 0, []
    for b in range(blocks):
        slots.append(jnp.where(flags[b] == 1, ones, count + zeros))
        ones, zeros = ones + flags[b], zeros + (1 - flags[b])
    row_ids = lax.broadcasted_iota(jnp.int32, (META, size), 0)
    meta = jnp.zeros((META, size), jnp.float32)
    for s in range(SLOTS):
        place = sum(jnp.where(slots[b] == s, b, 0) for b in range(blocks))
        row = pl.multiple_of(place // blk_cols * size, size)
        col = pl.multiple_of(place % blk_cols * size, size)
        block = weights_ref[pl.ds(row, size), pl.ds(col, size)]
        block = jnp.where(s < count, block, jnp.zeros_like(block))
        packet_ref[pl.ds(s * size, size), :] = block
        meta = jnp.where(row_ids == s, place.astype(jnp.float32), meta)
    packet_ref[pl.ds(SLOTS * size, META), :] = meta.astype(packet_ref.dtype)


def sums_kernel(blk_cols, *refs):
    *packet_refs, sums_ref = refs
    size = packet_refs[0].shape[1]
    sums_ref[...] = jnp.zeros_like(sums_ref)
    for m, ref in enumerate(packet_refs):
        for s, place in enumerate(places_in(ref, size)):
            col = pl.multiple_of(place % blk_cols * size, size)
            block = ref[pl.ds(s * size, size), :].astype(jnp.float32)
            sums_ref[m : m + 1, pl.ds(col, size)] += jnp.sum(block, axis=0, keepdims=True)


def expand_kernel(gr_size, gc_size, blk_rows, blk_cols, *refs):
    out_flags_ref, totals_ref = refs[:2]
    left_refs = refs[2 : 2 + gr_size]
    right_refs = refs[2 + gr_size : 2 + gr_size + gc_size]
    inflated_ref, sums_ref, left, right = refs[2 + gr_size + gc_size :]
    size = left.shape[0] // blk_rows
    my_col, my_row = lax.axis_index("gr"), lax.axis_index("gc")

    inverse = 1.0 / totals_ref[...]
    left[...] = jnp.zeros_like(left)
    right[...] = jnp.zeros_like(right)
    for m, ref in enumerate(left_refs):
        base = (my_col ^ m) * blk_cols
        for s, place in enumerate(places_in(ref, size)):
            row = pl.multiple_of(place // blk_cols * size, size)
            col = place % blk_cols
            scale = inverse[m : m + 1, :size]
            for j in range(1, blk_cols):
                scale = jnp.where(col == j, inverse[m : m + 1, j * size : (j + 1) * size], scale)
            block = ref[pl.ds(s * size, size), :].astype(jnp.float32) * scale
            at = pl.multiple_of((base + col) * size, size)
            left[pl.ds(row, size), pl.ds(at, size)] = block.astype(left.dtype)
    for m, ref in enumerate(right_refs):
        base = (my_row ^ m) * blk_rows
        for s, place in enumerate(places_in(ref, size)):
            row = pl.multiple_of((base + place // blk_cols) * size, size)
            col = pl.multiple_of(place % blk_cols * size, size)
            right[pl.ds(row, size), pl.ds(col, size)] = ref[pl.ds(s * size, size), :]
    product = jnp.dot(left[...], right[...], preferred_element_type=jnp.float32)
    for j in range(blk_cols):
        at = slice(j * size, (j + 1) * size)
        total = jnp.zeros((1, size), jnp.float32)
        for i in range(blk_rows):
            rows = slice(i * size, (i + 1) * size)
            kept = product[rows, at] * inverse[0:1, at]
            kept = kept * out_flags_ref[i, j].astype(jnp.float32)
            squared = kept * kept
            inflated_ref[rows, at] = squared
            total = total + jnp.sum(squared, axis=0, keepdims=True)
        sums_ref[:, at] = total


def shards(weights, in_pattern, out_pattern):
    blk_rows, blk_cols = in_pattern.shape
    local_rows, local_cols = weights.shape
    size = local_rows // blk_rows
    gr_size, gc_size = lax.axis_size("gr"), lax.axis_size("gc")
    order_size = local_rows * gc_size
    small = pltpu.CompilerParams(vmem_limit_bytes=8 << 20)
    packet = pl.pallas_call(
        pack_kernel,
        out_shape=jax.ShapeDtypeStruct((SLOTS * size + META, size), weights.dtype),
        in_specs=[SMEM, VMEM],
        out_specs=VMEM,
        compiler_params=small,
        name="pack",
    )(in_pattern, weights)
    right = gather_xor(packet, "gc")
    left = gather_xor(packet, "gr")
    totals = pl.pallas_call(
        functools.partial(sums_kernel, blk_cols),
        out_shape=jax.ShapeDtypeStruct((2, local_cols), jnp.float32),
        in_specs=[VMEM, VMEM],
        out_specs=VMEM,
        compiler_params=small,
        name="sums",
    )(*left[:2])
    for bit in reversed(bits_of(gr_size)[:-1]):
        totals = jnp.concatenate([totals, swap(totals, "gr", bit)], axis=0)
    totals = total_over(totals, "gc")
    inflated, sums = pl.pallas_call(
        functools.partial(expand_kernel, gr_size, gc_size, blk_rows, blk_cols),
        out_shape=(
            jax.ShapeDtypeStruct((local_rows, local_cols), jnp.float32),
            jax.ShapeDtypeStruct((1, local_cols), jnp.float32),
        ),
        in_specs=[SMEM, VMEM] + [VMEM] * (gr_size + gc_size),
        out_specs=(VMEM, VMEM),
        scratch_shapes=[
            pltpu.VMEM((local_rows, order_size), jnp.bfloat16),
            pltpu.VMEM((order_size, local_cols), jnp.bfloat16),
        ],
        compiler_params=pltpu.CompilerParams(vmem_limit_bytes=40 << 20),
        name="expand",
    )(out_pattern, totals, *left, *right)
    output_total = total_at_once(sums, "gc")
    return (inflated / output_total * float(order_size)).astype(jnp.bfloat16)


def solution(mesh):
    in_specs = (P("gc", "gr"), P("gc", "gr"), P("gc", "gr"))
    out_specs = P("gc", "gr")
    return jax.shard_map(shards, mesh=mesh, in_specs=in_specs, out_specs=out_specs, check_vma=False)
```

```python
import functools

import jax
import jax.numpy as jnp
from jax import lax
from jax.experimental import pallas as pl
from jax.experimental.pallas import tpu as pltpu
from jax.sharding import PartitionSpec as P

SLOTS = 4
META = 16
VMEM = pl.BlockSpec(memory_space=pltpu.VMEM)
SMEM = pl.BlockSpec(memory_space=pltpu.SMEM)
HBM = pl.BlockSpec(memory_space=pltpu.HBM)
SMALL = pltpu.CompilerParams(vmem_limit_bytes=16 << 20)


def bits_of(size):
    return [1 << b for b in reversed(range(size.bit_length() - 1))]


def swap(x, axis, mask):
    return lax.ppermute(x, axis, [(i, i ^ mask) for i in range(lax.axis_size(axis))])


def in_hbm(x):
    return pltpu.with_memory_space_constraint(x, pltpu.HBM)


def way_to(mask, axis):
    full = lax.axis_size(axis) - 1
    if mask == full and mask.bit_count() > 2:
        return 1, mask ^ 1
    bits = [bit for bit in bits_of(full + 1) if mask & bit]
    last = bits[min(1, len(bits) - 1)]
    return mask ^ last, last


def total_at_once(x, axis):
    size = lax.axis_size(axis)
    parts = lax.all_to_all(jnp.broadcast_to(x[None], (size,) + x.shape), axis, 0, 0)
    return jnp.sum(parts, axis=0)


def places_in(packet_ref, size):
    meta = packet_ref[pl.ds(SLOTS * size, META), :].astype(jnp.float32)
    return [jnp.max(meta[s : s + 1, :]).astype(jnp.int32) for s in range(SLOTS)]


def add_sums(packet_ref, sums_ref, at, blk_cols):
    size = packet_ref.shape[1]
    for s, place in enumerate(places_in(packet_ref, size)):
        col = pl.multiple_of(place % blk_cols * size, size)
        block = packet_ref[pl.ds(s * size, size), :].astype(jnp.float32)
        sums_ref[at : at + 1, pl.ds(col, size)] += jnp.sum(block, axis=0, keepdims=True)


def pack_kernel(flags_hbm, weights_hbm, packet_ref, sums_ref, flags_ref, weights_ref, sems):
    copies = [
        pltpu.make_async_copy(flags_hbm, flags_ref, sems.at[0]),
        pltpu.make_async_copy(weights_hbm, weights_ref, sems.at[1]),
    ]
    for copy in copies:
        copy.start()
    for copy in copies:
        copy.wait()
    blk_rows, blk_cols = flags_ref.shape
    size = weights_ref.shape[0] // blk_rows
    blocks = blk_rows * blk_cols
    flags = [flags_ref[b // blk_cols, b % blk_cols] for b in range(blocks)]
    count = sum(flags)
    ones, zeros, slots = 0, 0, []
    for b in range(blocks):
        slots.append(jnp.where(flags[b] == 1, ones, count + zeros))
        ones, zeros = ones + flags[b], zeros + (1 - flags[b])
    sums_ref[...] = jnp.zeros_like(sums_ref)
    row_ids = lax.broadcasted_iota(jnp.int32, (META, size), 0)
    meta = jnp.zeros((META, size), jnp.float32)
    for s in range(SLOTS):
        place = sum(jnp.where(slots[b] == s, b, 0) for b in range(blocks))
        row = pl.multiple_of(place // blk_cols * size, size)
        col = pl.multiple_of(place % blk_cols * size, size)
        block = weights_ref[pl.ds(row, size), pl.ds(col, size)]
        block = jnp.where(s < count, block, jnp.zeros_like(block))
        packet_ref[0, pl.ds(s * size, size), :] = block
        sums_ref[:, pl.ds(col, size)] += jnp.sum(block.astype(jnp.float32), axis=0, keepdims=True)
        meta = jnp.where(row_ids == s, place.astype(jnp.float32), meta)
    packet_ref[0, pl.ds(SLOTS * size, META), :] = meta.astype(packet_ref.dtype)


def relay_kernel(blk_cols, held, routes, *refs):
    sent_refs, sums_ref = refs[-len(routes) - 1 : -1], refs[-1]
    sums_ref[...] = refs[0][...]
    for n in held:
        add_sums(refs[1 + n].at[0], sums_ref, 0, blk_cols)
    for sent_ref, route in zip(sent_refs, routes):
        for at, source in enumerate(route):
            sent_ref[at] = refs[1 + source][0]


def total_of_halves(sums):
    gr_size, gc_size = lax.axis_size("gr"), lax.axis_size("gc")
    groups = [
        [r * gc_size + c for r in range(gr_size) for c in (i, i ^ (gc_size - 1))]
        for i in range(gc_size // 2)
    ]
    parts = jnp.broadcast_to(sums[None], (2 * gr_size,) + sums.shape)
    parts = lax.all_to_all(parts, ("gr", "gc"), 0, 0, axis_index_groups=groups)
    return jnp.sum(parts.reshape(gr_size, 2, -1), axis=1)


def spread(blk_rows, blk_cols, left_refs, right_refs, left, right):
    size = left.shape[0] // blk_rows
    my_col, my_row = lax.axis_index("gr"), lax.axis_index("gc")
    for m, ref in left_refs.items():
        for s, place in enumerate(places_in(ref, size)):
            row = pl.multiple_of(place // blk_cols * size, size)
            at = pl.multiple_of(((my_col ^ m) * blk_cols + place % blk_cols) * size, size)
            left[pl.ds(row, size), pl.ds(at, size)] = ref[pl.ds(s * size, size), :]
    for m, ref in right_refs.items():
        base = (my_row ^ m) * blk_rows
        for s, place in enumerate(places_in(ref, size)):
            row = pl.multiple_of((base + place // blk_cols) * size, size)
            col = pl.multiple_of(place % blk_cols * size, size)
            right[pl.ds(row, size), pl.ds(col, size)] = ref[pl.ds(s * size, size), :]


def spread_kernel(blk_rows, blk_cols, left_at, right_at, *refs):
    left, right = refs[-2:]
    left[...] = jnp.zeros_like(left)
    right[...] = jnp.zeros_like(right)
    left_refs = {m: refs[n].at[at] for m, (n, at) in left_at.items()}
    right_refs = {m: refs[n].at[at] for m, (n, at) in right_at.items()}
    spread(blk_rows, blk_cols, left_refs, right_refs, left, right)


def expand_kernel(flags_hbm, totals_ref, left, right, inflated_ref, sums_ref, flags_ref, scaled, sem):
    copy = pltpu.make_async_copy(flags_hbm, flags_ref, sem)
    copy.start()
    blk_rows, blk_cols = flags_ref.shape
    size = left.shape[0] // blk_rows
    width = totals_ref.shape[1]
    inverse = 1.0 / totals_ref[...]
    for m in range(totals_ref.shape[0]):
        at = slice(m * width, (m + 1) * width)
        scaled[:, at] = (left[:, at].astype(jnp.float32) * inverse[m : m + 1]).astype(scaled.dtype)
    own = 1.0 / totals_ref[pl.ds(lax.axis_index("gr"), 1), :]
    product = jnp.dot(scaled[...], right[...], preferred_element_type=jnp.float32)
    copy.wait()
    for j in range(blk_cols):
        at = slice(j * size, (j + 1) * size)
        total = jnp.zeros((1, size), jnp.float32)
        for i in range(blk_rows):
            rows = slice(i * size, (i + 1) * size)
            kept = product[rows, at] * own[:, at]
            kept = kept * flags_ref[i, j].astype(jnp.float32)
            squared = kept * kept
            inflated_ref[rows, at] = squared
            total = total + jnp.sum(squared, axis=0, keepdims=True)
        sums_ref[:, at] = total


def shards(weights, in_pattern, out_pattern):
    blk_rows, blk_cols = in_pattern.shape
    local_rows, local_cols = weights.shape
    size = local_rows // blk_rows
    gr_size, gc_size = lax.axis_size("gr"), lax.axis_size("gc")
    order_size = local_rows * gc_size
    sums_shape = jax.ShapeDtypeStruct((1, local_cols), jnp.float32)
    packet, sums = pl.pallas_call(
        pack_kernel,
        out_shape=(jax.ShapeDtypeStruct((1, SLOTS * size + META, size), weights.dtype), sums_shape),
        in_specs=[HBM, HBM],
        out_specs=(VMEM, VMEM),
        scratch_shapes=[
            pltpu.SMEM(in_pattern.shape, in_pattern.dtype),
            pltpu.VMEM(weights.shape, weights.dtype),
            pltpu.SemaphoreType.DMA((2,)),
        ],
        compiler_params=SMALL,
        name="pack",
    )(in_hbm(in_pattern), in_hbm(weights))
    full = gc_size - 1
    arrays, right_at, left_at = [packet], {0: (0, 0)}, {0: (0, 0)}

    def keep(array, table, masks):
        arrays.append(array)
        table.update({m: (len(arrays) - 1, at) for at, m in enumerate(masks)})

    for bit in bits_of(gc_size):
        keep(swap(packet, "gc", bit), right_at, [bit])
    for bit in bits_of(gr_size)[:-1]:
        keep(swap(packet, "gr", bit), left_at, [bit])
    hops = {}
    later = [m for m in range(gc_size) if m not in right_at]
    for mask in later:
        if min(mask.bit_count(), max(2, full.bit_count() - 1)) == 2:
            parent, hop = way_to(mask, "gc")
            hops.setdefault(hop, []).append((mask, parent))
    evens = sorted(left_at)
    routes = [[right_at[parent][0] for _, parent in hop] for hop in hops.values()]
    routes.append([left_at[m][0] for m in evens])
    *sent, sums = pl.pallas_call(
        functools.partial(relay_kernel, blk_cols, range(1, len(right_at)), routes),
        out_shape=[jax.ShapeDtypeStruct((len(r),) + packet.shape[1:], packet.dtype) for r in routes]
        + [sums_shape],
        in_specs=[VMEM] * (1 + len(arrays)),
        out_specs=[VMEM] * (1 + len(routes)),
        compiler_params=SMALL,
        name="relay",
    )(sums, *arrays)
    for (hop, masks), buffer in zip(hops.items(), sent):
        keep(swap(buffer, "gc", hop), right_at, [m for m, _ in masks])
    keep(swap(sent[-1], "gr", 1), left_at, [m | 1 for m in evens])
    totals = total_of_halves(sums)
    left, right = pl.pallas_call(
        functools.partial(spread_kernel, blk_rows, blk_cols, left_at, right_at),
        out_shape=(
            jax.ShapeDtypeStruct((local_rows, order_size), weights.dtype),
            jax.ShapeDtypeStruct((order_size, local_cols), weights.dtype),
        ),
        in_specs=[VMEM] * len(arrays),
        out_specs=(VMEM, VMEM),
        compiler_params=SMALL,
        name="spread",
    )(*arrays)
    inflated, sums = pl.pallas_call(
        expand_kernel,
        out_shape=(jax.ShapeDtypeStruct(weights.shape, jnp.float32), sums_shape),
        in_specs=[HBM] + [VMEM] * 3,
        out_specs=(VMEM, VMEM),
        scratch_shapes=[
            pltpu.SMEM(out_pattern.shape, out_pattern.dtype),
            pltpu.VMEM((local_rows, order_size), weights.dtype),
            pltpu.SemaphoreType.DMA,
        ],
        compiler_params=SMALL,
        name="expand",
    )(in_hbm(out_pattern), totals, left, right)
    output_total = total_at_once(sums, "gc")
    return (inflated / output_total * float(order_size)).astype(jnp.bfloat16)


def solution(mesh):
    in_specs = (P("gc", "gr"), P("gc", "gr"), P("gc", "gr"))
    out_specs = P("gc", "gr")
    return jax.shard_map(shards, mesh=mesh, in_specs=in_specs, out_specs=out_specs, check_vma=False)
```

```python
import functools

import jax
import jax.numpy as jnp
from jax import lax
from jax.experimental import pallas as pl
from jax.experimental.pallas import tpu as pltpu
from jax.sharding import PartitionSpec as P

SLOTS = 4
META = 16
VMEM = pl.BlockSpec(memory_space=pltpu.VMEM)
HBM = pl.BlockSpec(memory_space=pltpu.HBM)
PARAMS = pltpu.CompilerParams(vmem_limit_bytes=16 << 20)
LONG = pl.CostEstimate(flops=10**10, bytes_accessed=0, transcendentals=0)


def in_hbm(x):
    return pltpu.with_memory_space_constraint(x, pltpu.HBM)


def bits_of(size):
    return [1 << b for b in reversed(range(size.bit_length() - 1))]


def swap(x, axis, mask):
    return lax.ppermute(x, axis, [(i, i ^ mask) for i in range(lax.axis_size(axis))])


def way_to(mask, axis):
    full = lax.axis_size(axis) - 1
    if mask == full and mask.bit_count() > 2:
        return 1, mask ^ 1
    bits = [bit for bit in bits_of(full + 1) if mask & bit]
    last = bits[min(1, len(bits) - 1)]
    return mask ^ last, last


def total_at_once(x, axis):
    size = lax.axis_size(axis)
    parts = lax.all_to_all(jnp.broadcast_to(x[None], (size,) + x.shape), axis, 0, 0)
    return jnp.sum(parts, axis=0)


def places_in(packet, size):
    meta = packet[pl.ds(SLOTS * size, META), :].astype(jnp.float32)
    return [jnp.max(meta[s : s + 1, :]).astype(jnp.int32) for s in range(SLOTS)]


def pack_kernel(flags_hbm, weights_hbm, packet_ref, sums_ref, flags_ref, weights_ref, sems):
    copies = [
        pltpu.make_async_copy(flags_hbm, flags_ref, sems.at[0]),
        pltpu.make_async_copy(weights_hbm, weights_ref, sems.at[1]),
    ]
    for copy in copies:
        copy.start()
    for copy in copies:
        copy.wait()
    blk_rows, blk_cols = flags_ref.shape
    size = weights_ref.shape[0] // blk_rows
    blocks = blk_rows * blk_cols
    flags = [flags_ref[b // blk_cols, b % blk_cols] for b in range(blocks)]
    count = sum(flags)
    ones, zeros, slots = 0, 0, []
    for b in range(blocks):
        slots.append(jnp.where(flags[b] == 1, ones, count + zeros))
        ones, zeros = ones + flags[b], zeros + (1 - flags[b])
    sums_ref[...] = jnp.zeros_like(sums_ref)
    row_ids = lax.broadcasted_iota(jnp.int32, (META, size), 0)
    meta = jnp.zeros((META, size), jnp.float32)
    for s in range(SLOTS):
        place = sum(jnp.where(slots[b] == s, b, 0) for b in range(blocks))
        row = pl.multiple_of(place // blk_cols * size, size)
        col = pl.multiple_of(place % blk_cols * size, size)
        block = weights_ref[pl.ds(row, size), pl.ds(col, size)]
        block = jnp.where(s < count, block, jnp.zeros_like(block))
        packet_ref[pl.ds(s * size, size), :] = block
        sums_ref[:, pl.ds(col, size)] += jnp.sum(block.astype(jnp.float32), axis=0, keepdims=True)
        meta = jnp.where(row_ids == s, place.astype(jnp.float32), meta)
    packet_ref[pl.ds(SLOTS * size, META), :] = meta.astype(packet_ref.dtype)


def rows_of(sums_ref):
    size = 128
    parts = [
        sums_ref[r : r + 1, at : at + size]
        for r in range(sums_ref.shape[0])
        for at in range(0, sums_ref.shape[1], size)
    ]
    return jnp.concatenate(parts, axis=0)


def split(x):
    high = x.astype(jnp.bfloat16)
    return high, (x - high.astype(jnp.float32)).astype(jnp.bfloat16)


def add_kernel(one_ref, other_ref, out_ref):
    out_ref[...] = one_ref[...] + other_ref[...]


def relay_kernel(routes, riding, sums_ref, *refs):
    packet_refs, sent_refs = refs[: -len(routes)], refs[-len(routes) :]
    rows = packet_refs[0].shape[0]
    if riding:
        high, low = split(rows_of(sums_ref))
    for sent_ref, (route, rider) in zip(sent_refs, routes):
        for at, source in enumerate(route):
            sent_ref[pl.ds(at * rows, rows), :] = packet_refs[source][...]
        if rider:
            first = len(route) * rows
            sent_ref[pl.ds(first, high.shape[0]), :] = high
            sent_ref[pl.ds(first + high.shape[0], high.shape[0]), :] = low


def spread(blk_rows, blk_cols, size, packets, right):
    my_row = lax.axis_index("gc")
    for m, packet in packets.items():
        base = (my_row ^ m) * blk_rows
        for s, place in enumerate(places_in(packet, size)):
            row = pl.multiple_of((base + place // blk_cols) * size, size)
            col = pl.multiple_of(place % blk_cols * size, size)
            right[pl.ds(row, size), pl.ds(col, size)] = packet[pl.ds(s * size, size), :]


def packets_in(refs, table, rows):
    return {m: refs[n].at[pl.ds(at * rows, rows), :] for m, (n, at) in table.items()}


def spread_kernel(blk_rows, blk_cols, evens, right_at, lefts_ref, *refs):
    *refs, right, left = refs
    rows, size = refs[0].shape
    right[...] = jnp.zeros_like(right)
    left[...] = jnp.zeros_like(left)
    spread(blk_rows, blk_cols, size, packets_in(refs, right_at, rows), right)
    my_col = lax.axis_index("gr")
    for n in range(lefts_ref.shape[0] // rows):
        packet = lefts_ref.at[pl.ds(n * rows, rows), :]
        gr = my_col // 2 * 2 + n // len(evens) ^ evens[n % len(evens)]
        for s, place in enumerate(places_in(packet, size)):
            row = pl.multiple_of(place // blk_cols * size, size)
            at = pl.multiple_of((gr * blk_cols + place % blk_cols) * size, size)
            left[pl.ds(row, size), pl.ds(at, size)] = packet[pl.ds(s * size, size), :]


def expand_kernel(right_at, riders, flags_hbm, sums_ref, left, *refs):
    *refs, _, inflated_ref, total_ref, right, flags_ref, scaled, sem = refs
    copy = pltpu.make_async_copy(flags_hbm, flags_ref, sem)
    copy.start()
    blk_rows, blk_cols = flags_ref.shape
    rows, size = refs[0].shape
    spread(blk_rows, blk_cols, size, packets_in(refs, right_at, rows), right)
    sums = rows_of(sums_ref)
    for n, at in riders:
        high = refs[n][pl.ds(at * rows, sums.shape[0]), :].astype(jnp.float32)
        low = refs[n][pl.ds(at * rows + sums.shape[0], sums.shape[0]), :].astype(jnp.float32)
        sums = sums + (high + low)
    inverse = 1.0 / sums
    for n in range(sums.shape[0]):
        at = slice(n * size, (n + 1) * size)
        scaled[:, at] = (left[:, at].astype(jnp.float32) * inverse[n : n + 1]).astype(scaled.dtype)
    product = jnp.dot(scaled[...], right[...], preferred_element_type=jnp.float32)
    copy.wait()
    my_col = lax.axis_index("gr")
    for j in range(blk_cols):
        at = slice(j * size, (j + 1) * size)
        own = inverse[j : j + 1]
        for r in range(1, sums.shape[0] // blk_cols):
            own = jnp.where(my_col == r, inverse[r * blk_cols + j : r * blk_cols + j + 1], own)
        total = jnp.zeros((1, size), jnp.float32)
        for i in range(blk_rows):
            rows_at = slice(i * size, (i + 1) * size)
            kept = product[rows_at, at] * own
            kept = kept * flags_ref[i, j].astype(jnp.float32)
            squared = kept * kept
            inflated_ref[rows_at, at] = squared
            total = total + jnp.sum(squared, axis=0, keepdims=True)
        total_ref[:, at] = total


def shards(weights, in_pattern, out_pattern):
    blk_rows, blk_cols = in_pattern.shape
    local_rows, local_cols = weights.shape
    size = local_rows // blk_rows
    gr_size, gc_size = lax.axis_size("gr"), lax.axis_size("gc")
    order_size = local_rows * gc_size
    sums_shape = jax.ShapeDtypeStruct((1, local_cols), jnp.float32)
    rows = SLOTS * size + META
    packet, sums = pl.pallas_call(
        pack_kernel,
        out_shape=(jax.ShapeDtypeStruct((rows, size), weights.dtype), sums_shape),
        in_specs=[HBM, HBM],
        out_specs=(VMEM, VMEM),
        scratch_shapes=[
            pltpu.SMEM(in_pattern.shape, in_pattern.dtype),
            pltpu.VMEM(weights.shape, weights.dtype),
            pltpu.SemaphoreType.DMA((2,)),
        ],
        compiler_params=PARAMS,
        name="pack",
    )(in_hbm(in_pattern), in_hbm(weights))

    arrays, right_at, evens = [packet], {0: (0, 0)}, {0: 0}

    def keep(array, masks):
        arrays.append(array)
        right_at.update({m: (len(arrays) - 1, at) for at, m in enumerate(masks)})

    riding = gc_size == 8
    if riding:
        sums = pl.pallas_call(
            add_kernel,
            out_shape=sums_shape,
            in_specs=[VMEM] * 2,
            out_specs=VMEM,
            compiler_params=PARAMS,
            cost_estimate=LONG,
            name="add",
        )(sums, swap(sums, "gc", 5))
    else:
        sums = lax.psum(sums, "gc")
    for bit in reversed(bits_of(gc_size)):
        keep(swap(packet, "gc", bit), [bit])
    for bit in bits_of(gr_size)[:-1]:
        for m, n in list(evens.items()):
            arrays.append(swap(arrays[n], "gr", bit))
            evens[m | bit] = len(arrays) - 1
    sums = lax.all_gather(sums, "gr", tiled=True)

    hops = {}
    for mask in range(gc_size):
        if mask not in right_at and min(mask.bit_count(), max(2, gc_size.bit_length() - 2)) == 2:
            parent, hop = way_to(mask, "gc")
            hops.setdefault(hop, []).append((mask, parent))
    routes = [([right_at[parent][0] for _, parent in hop], riding) for hop in hops.values()]
    routes.append((list(evens.values()), False))
    extra = 2 * gr_size * blk_cols
    sent = pl.pallas_call(
        functools.partial(relay_kernel, routes, riding),
        out_shape=[
            jax.ShapeDtypeStruct((len(route) * rows + extra * rider, size), packet.dtype)
            for route, rider in routes
        ],
        in_specs=[VMEM] * (1 + len(arrays)),
        out_specs=[VMEM] * len(routes),
        compiler_params=PARAMS,
        name="relay",
    )(sums, *arrays)
    cores = [[i, i + 1] for i in range(0, gr_size, 2)]
    lefts = lax.all_gather(sent[-1], "gr", axis_index_groups=cores, tiled=True)
    right, left = pl.pallas_call(
        functools.partial(spread_kernel, blk_rows, blk_cols, list(evens), dict(right_at)),
        out_shape=(
            jax.ShapeDtypeStruct((order_size, local_cols), weights.dtype),
            jax.ShapeDtypeStruct((local_rows, order_size), weights.dtype),
        ),
        in_specs=[VMEM] * (1 + len(arrays)),
        out_specs=(VMEM, VMEM),
        compiler_params=PARAMS,
        name="spread",
    )(lefts, *arrays)
    early, riders = set(right_at), []
    for (hop, masks), buffer in zip(hops.items(), sent):
        keep(swap(buffer, "gc", hop), [m for m, _ in masks])
        if riding:
            riders.append((len(arrays) - 1, len(masks)))
    for mask in sorted(set(range(gc_size)) - set(right_at), key=lambda m: m.bit_count()):
        parent, hop = way_to(mask, "gc")
        n, at = right_at[parent]
        keep(swap(arrays[n][at * rows : (at + 1) * rows], "gc", hop), [mask])
    late_at = {m: at for m, at in right_at.items() if m not in early}
    inflated, sums, _ = pl.pallas_call(
        functools.partial(expand_kernel, late_at, riders),
        out_shape=(jax.ShapeDtypeStruct(weights.shape, jnp.float32), sums_shape, right),
        in_specs=[HBM] + [VMEM] * (3 + len(arrays)),
        out_specs=(VMEM, VMEM, VMEM),
        input_output_aliases={3 + len(arrays): 2},
        scratch_shapes=[
            pltpu.SMEM(out_pattern.shape, out_pattern.dtype),
            pltpu.VMEM((local_rows, order_size), weights.dtype),
            pltpu.SemaphoreType.DMA,
        ],
        compiler_params=PARAMS,
        name="expand",
    )(in_hbm(out_pattern), sums, left, *arrays, right)
    output_total = total_at_once(sums, "gc")
    return (inflated / output_total * float(order_size)).astype(jnp.bfloat16)


def solution(mesh):
    in_specs = (P("gc", "gr"), P("gc", "gr"), P("gc", "gr"))
    out_specs = P("gc", "gr")
    return jax.shard_map(shards, mesh=mesh, in_specs=in_specs, out_specs=out_specs, check_vma=False)
```

```python
import functools

import jax
import jax.numpy as jnp
from jax import lax
from jax.experimental import pallas as pl
from jax.experimental.pallas import tpu as pltpu
from jax.sharding import PartitionSpec as P

SLOTS = 4
META = 16
VMEM = pl.BlockSpec(memory_space=pltpu.VMEM)
HBM = pl.BlockSpec(memory_space=pltpu.HBM)
PARAMS = pltpu.CompilerParams(vmem_limit_bytes=16 << 20)
LONG = pl.CostEstimate(flops=10**10, bytes_accessed=0, transcendentals=0)


def in_hbm(x):
    return pltpu.with_memory_space_constraint(x, pltpu.HBM)


def bits_of(size):
    return [1 << b for b in reversed(range(size.bit_length() - 1))]


def swap(x, axis, mask):
    return lax.ppermute(x, axis, [(i, i ^ mask) for i in range(lax.axis_size(axis))])


def with_partner(x, axis, mask):
    return jnp.concatenate([x, swap(x, axis, mask)], axis=0)


def way_to(mask, axis):
    full = lax.axis_size(axis) - 1
    if mask == full and mask.bit_count() > 2:
        return 1, mask ^ 1
    bits = [bit for bit in bits_of(full + 1) if mask & bit]
    last = bits[min(1, len(bits) - 1)]
    return mask ^ last, last


def places_in(packet, size):
    meta = packet[pl.ds(SLOTS * size, META), :].astype(jnp.float32)
    return [jnp.max(meta[s : s + 1, :]).astype(jnp.int32) for s in range(SLOTS)]


def pack_kernel(flags_hbm, kept_hbm, weights_hbm, packet_ref, sums_ref, flags_ref, kept_ref, weights_ref, sems):
    copies = [
        pltpu.make_async_copy(flags_hbm, flags_ref, sems.at[0]),
        pltpu.make_async_copy(kept_hbm, kept_ref, sems.at[1]),
        pltpu.make_async_copy(weights_hbm, weights_ref, sems.at[2]),
    ]
    for copy in copies:
        copy.start()
    for copy in copies:
        copy.wait()
    blk_rows, blk_cols = flags_ref.shape
    size = weights_ref.shape[0] // blk_rows
    blocks = blk_rows * blk_cols
    flags = [flags_ref[b // blk_cols, b % blk_cols] for b in range(blocks)]
    count = sum(flags)
    ones, zeros, slots = 0, 0, []
    for b in range(blocks):
        slots.append(jnp.where(flags[b] == 1, ones, count + zeros))
        ones, zeros = ones + flags[b], zeros + (1 - flags[b])
    sums_ref[...] = jnp.zeros_like(sums_ref)
    row_ids = lax.broadcasted_iota(jnp.int32, (META, size), 0)
    meta = jnp.zeros((META, size), jnp.float32)
    for s in range(SLOTS):
        place = sum(jnp.where(slots[b] == s, b, 0) for b in range(blocks))
        row = pl.multiple_of(place // blk_cols * size, size)
        col = pl.multiple_of(place % blk_cols * size, size)
        block = weights_ref[pl.ds(row, size), pl.ds(col, size)]
        block = jnp.where(s < count, block, jnp.zeros_like(block))
        packet_ref[pl.ds(s * size, size), :] = block
        sums_ref[:, pl.ds(col, size)] += jnp.sum(block.astype(jnp.float32), axis=0, keepdims=True)
        meta = jnp.where(row_ids == s, place.astype(jnp.float32), meta)
    for b in range(blocks):
        kept = kept_ref[b // blk_cols, b % blk_cols].astype(jnp.float32)
        meta = jnp.where(row_ids == SLOTS + b, kept, meta)
    packet_ref[pl.ds(SLOTS * size, META), :] = meta.astype(packet_ref.dtype)


def rows_of(sums_ref):
    size = 128
    parts = [
        sums_ref[r : r + 1, at : at + size]
        for r in range(sums_ref.shape[0])
        for at in range(0, sums_ref.shape[1], size)
    ]
    return jnp.concatenate(parts, axis=0)


def split(x):
    high = x.astype(jnp.bfloat16)
    return high, (x - high.astype(jnp.float32)).astype(jnp.bfloat16)


def add_kernel(one_ref, other_ref, out_ref):
    out_ref[...] = one_ref[...] + other_ref[...]


def relay_kernel(routes, riding, sums_ref, *refs):
    packet_refs, sent_refs = refs[: -len(routes)], refs[-len(routes) :]
    rows = packet_refs[0].shape[0]
    if riding:
        high, low = split(rows_of(sums_ref))
    for sent_ref, (route, rider) in zip(sent_refs, routes):
        for at, source in enumerate(route):
            sent_ref[pl.ds(at * rows, rows), :] = packet_refs[source][...]
        if rider:
            first = len(route) * rows
            sent_ref[pl.ds(first, high.shape[0]), :] = high
            sent_ref[pl.ds(first + high.shape[0], high.shape[0]), :] = low


def spread(blk_rows, blk_cols, size, packets, right):
    my_row = lax.axis_index("gc")
    for m, packet in packets.items():
        base = (my_row ^ m) * blk_rows
        for s, place in enumerate(places_in(packet, size)):
            row = pl.multiple_of((base + place // blk_cols) * size, size)
            col = pl.multiple_of(place % blk_cols * size, size)
            right[pl.ds(row, size), pl.ds(col, size)] = packet[pl.ds(s * size, size), :]


def packets_in(refs, table, rows):
    return {m: refs[n].at[pl.ds(at * rows, rows), :] for m, (n, at) in table.items()}


def spread_kernel(blk_rows, blk_cols, right_at, *refs):
    *refs, right, left = refs
    rows, size = refs[0].shape
    right[...] = jnp.zeros_like(right)
    left[...] = jnp.zeros_like(left)
    spread(blk_rows, blk_cols, size, packets_in(refs, right_at, rows), right)


def expand_kernel(right_at, riders, evens, blk_cols, sums_ref, *refs):
    *halves, _, _, inflated_ref, total_ref, right, left = refs[:2] + refs[-6:]
    refs = refs[2:-6]
    rows, size = refs[0].shape
    blk_rows = inflated_ref.shape[0] // size
    spread(blk_rows, blk_cols, size, packets_in(refs, right_at, rows), right)
    sums = rows_of(sums_ref)
    for n, at in riders:
        high = refs[n][pl.ds(at * rows, sums.shape[0]), :].astype(jnp.float32)
        low = refs[n][pl.ds(at * rows + sums.shape[0], sums.shape[0]), :].astype(jnp.float32)
        sums = sums + (high + low)
    inverse = 1.0 / sums
    my_col = lax.axis_index("gr")
    for n in range(2 * len(evens)):
        gr = my_col // 2 * 2 + n // len(evens) ^ evens[n % len(evens)]
        scales = []
        for j in range(blk_cols):
            scale = inverse[j : j + 1]
            for m in range(1, 2 * len(evens)):
                there = inverse[m * blk_cols + j : m * blk_cols + j + 1]
                scale = jnp.where(my_col ^ m == gr, there, scale)
            scales.append(scale)
        for part, half in enumerate(halves):
            packet = half.at[pl.ds(n * rows, rows), :]
            for s, place in enumerate(places_in(packet, size)):
                row = pl.multiple_of((part * blk_rows + place // blk_cols) * size, size)
                col = place % blk_cols
                scale = scales[0]
                for j in range(1, blk_cols):
                    scale = jnp.where(col == j, scales[j], scale)
                block = packet[pl.ds(s * size, size), :].astype(jnp.float32) * scale
                at = pl.multiple_of((gr * blk_cols + col) * size, size)
                left[pl.ds(row, size), pl.ds(at, size)] = block.astype(left.dtype)
    product = jnp.dot(left[...], right[...], preferred_element_type=jnp.float32)
    first = SLOTS * size
    flags = [ref[pl.ds(first, META), :].astype(jnp.float32) for ref in (refs[0], refs[1])]
    for j in range(blk_cols):
        at = slice(j * size, (j + 1) * size)
        own = inverse[j : j + 1]
        total = jnp.zeros((1, size), jnp.float32)
        for i in range(2 * blk_rows):
            part, flag = i // blk_rows, SLOTS + i % blk_rows * blk_cols + j
            kept = product[i * size : (i + 1) * size, at] * own
            kept = kept * flags[part][flag : flag + 1]
            squared = kept * kept
            if part == 0:
                inflated_ref[i * size : (i + 1) * size, at] = squared
            total = total + jnp.sum(squared, axis=0, keepdims=True)
        total_ref[:, at] = total


def shards(weights, in_pattern, out_pattern):
    blk_rows, blk_cols = in_pattern.shape
    local_rows, local_cols = weights.shape
    size = local_rows // blk_rows
    gr_size, gc_size = lax.axis_size("gr"), lax.axis_size("gc")
    order_size = local_rows * gc_size
    sums_shape = jax.ShapeDtypeStruct((1, local_cols), jnp.float32)
    rows = SLOTS * size + META
    packet, sums = pl.pallas_call(
        pack_kernel,
        out_shape=(jax.ShapeDtypeStruct((rows, size), weights.dtype), sums_shape),
        in_specs=[HBM] * 3,
        out_specs=(VMEM, VMEM),
        scratch_shapes=[
            pltpu.SMEM(in_pattern.shape, in_pattern.dtype),
            pltpu.SMEM(out_pattern.shape, out_pattern.dtype),
            pltpu.VMEM(weights.shape, weights.dtype),
            pltpu.SemaphoreType.DMA((3,)),
        ],
        compiler_params=PARAMS,
        name="pack",
    )(in_hbm(in_pattern), in_hbm(out_pattern), in_hbm(weights))

    arrays, right_at, evens = [packet], {0: (0, 0)}, {0: 0}

    def keep(array, masks):
        arrays.append(array)
        right_at.update({m: (len(arrays) - 1, at) for at, m in enumerate(masks)})

    riding = gc_size == 8
    sums = with_partner(sums, "gr", 1)
    if riding:
        sums = pl.pallas_call(
            add_kernel,
            out_shape=jax.ShapeDtypeStruct(sums.shape, sums.dtype),
            in_specs=[VMEM] * 2,
            out_specs=VMEM,
            compiler_params=PARAMS,
            cost_estimate=LONG,
            name="add",
        )(sums, swap(sums, "gc", 5))
    else:
        sums = lax.psum(sums, "gc")
    keep(swap(packet, "gc", 1), [1])
    for bit in bits_of(gr_size)[:-1]:
        for m, n in list(evens.items()):
            arrays.append(swap(arrays[n], "gr", bit))
            evens[m | bit] = len(arrays) - 1
    for bit in reversed(bits_of(gc_size)[:-1]):
        keep(swap(packet, "gc", bit), [bit])
    others = {0: right_at[1][0]}
    for m in list(evens)[1:]:
        arrays.append(swap(arrays[evens[m]], "gc", 1))
        others[m] = len(arrays) - 1
    for bit in reversed(bits_of(gr_size)[:-1]):
        sums = with_partner(sums, "gr", bit)

    hops = {}
    for mask in range(gc_size):
        if mask not in right_at and min(mask.bit_count(), max(2, gc_size.bit_length() - 2)) == 2:
            parent, hop = way_to(mask, "gc")
            hops.setdefault(hop, []).append((mask, parent))
    routes = [([right_at[parent][0] for _, parent in hop], riding) for hop in hops.values()]
    routes.append((list(evens.values()), False))
    routes.append((list(others.values()), False))
    extra = 2 * gr_size * blk_cols
    sent = pl.pallas_call(
        functools.partial(relay_kernel, routes, riding),
        out_shape=[
            jax.ShapeDtypeStruct((len(route) * rows + extra * rider, size), packet.dtype)
            for route, rider in routes
        ],
        in_specs=[VMEM] * (1 + len(arrays)),
        out_specs=[VMEM] * len(routes),
        compiler_params=PARAMS,
        name="relay",
    )(sums, *arrays)
    cores = [[i, i + 1] for i in range(0, gr_size, 2)]
    lefts = [
        lax.all_gather(half, "gr", axis_index_groups=cores, tiled=True) for half in sent[-2:]
    ]
    right, left = pl.pallas_call(
        functools.partial(spread_kernel, blk_rows, blk_cols, dict(right_at)),
        out_shape=(
            jax.ShapeDtypeStruct((order_size, local_cols), weights.dtype),
            jax.ShapeDtypeStruct((2 * local_rows, order_size), weights.dtype),
        ),
        in_specs=[VMEM] * len(arrays),
        out_specs=(VMEM, VMEM),
        compiler_params=PARAMS,
        name="spread",
    )(*arrays)
    early, riders = set(right_at), []
    for (hop, masks), buffer in zip(hops.items(), sent):
        keep(swap(buffer, "gc", hop), [m for m, _ in masks])
        if riding:
            riders.append((len(arrays) - 1, len(masks)))
    for mask in sorted(set(range(gc_size)) - set(right_at), key=lambda m: m.bit_count()):
        parent, hop = way_to(mask, "gc")
        n, at = right_at[parent]
        keep(swap(arrays[n][at * rows : (at + 1) * rows], "gc", hop), [mask])
    late_at = {m: at for m, at in right_at.items() if m not in early}
    inflated, sums, *_ = pl.pallas_call(
        functools.partial(expand_kernel, late_at, riders, list(evens), blk_cols),
        out_shape=(jax.ShapeDtypeStruct(weights.shape, jnp.float32), sums_shape, right, left),
        in_specs=[VMEM] * (5 + len(arrays)),
        out_specs=[VMEM] * 4,
        input_output_aliases={3 + len(arrays): 2, 4 + len(arrays): 3},
        compiler_params=PARAMS,
        name="expand",
    )(sums, *lefts, *arrays, right, left)
    output_total = sums
    for mask in range(2, gc_size, 2):
        output_total = output_total + swap(sums, "gc", mask)
    return (inflated / output_total * float(order_size)).astype(jnp.bfloat16)


def solution(mesh):
    in_specs = (P("gc", "gr"), P("gc", "gr"), P("gc", "gr"))
    out_specs = P("gc", "gr")
    return jax.shard_map(shards, mesh=mesh, in_specs=in_specs, out_specs=out_specs, check_vma=False)
```

```python
import functools

import jax
import jax.numpy as jnp
from jax import lax
from jax.experimental import pallas as pl
from jax.experimental.pallas import tpu as pltpu
from jax.sharding import PartitionSpec as P

SLOTS = 4
META = 16
VMEM = pl.BlockSpec(memory_space=pltpu.VMEM)
HBM = pl.BlockSpec(memory_space=pltpu.HBM)
PARAMS = pltpu.CompilerParams(vmem_limit_bytes=16 << 20)
LONG = pl.CostEstimate(flops=10**10, bytes_accessed=0, transcendentals=0)


def in_hbm(x):
    return pltpu.with_memory_space_constraint(x, pltpu.HBM)


def bits_of(size):
    return [1 << b for b in reversed(range(size.bit_length() - 1))]


def swap(x, axis, mask):
    return lax.ppermute(x, axis, [(i, i ^ mask) for i in range(lax.axis_size(axis))])


def way_to(mask, axis):
    full = lax.axis_size(axis) - 1
    if mask == full and mask.bit_count() > 2:
        return 1, mask ^ 1
    bits = [bit for bit in bits_of(full + 1) if mask & bit]
    last = bits[min(1, len(bits) - 1)]
    return mask ^ last, last


def places_in(packet, size):
    meta = packet[pl.ds(SLOTS * size, META), :].astype(jnp.float32)
    return [jnp.max(meta[s : s + 1, :]).astype(jnp.int32) for s in range(SLOTS)]


def pack_kernel(flags_hbm, kept_hbm, weights_hbm, packet_ref, sums_ref, flags_ref, kept_ref, weights_ref, sems):
    copies = [
        pltpu.make_async_copy(flags_hbm, flags_ref, sems.at[0]),
        pltpu.make_async_copy(kept_hbm, kept_ref, sems.at[1]),
        pltpu.make_async_copy(weights_hbm, weights_ref, sems.at[2]),
    ]
    for copy in copies:
        copy.start()
    for copy in copies:
        copy.wait()
    blk_rows, blk_cols = flags_ref.shape
    size = weights_ref.shape[0] // blk_rows
    blocks = blk_rows * blk_cols
    flags = [flags_ref[b // blk_cols, b % blk_cols] for b in range(blocks)]
    count = sum(flags)
    ones, zeros, slots = 0, 0, []
    for b in range(blocks):
        slots.append(jnp.where(flags[b] == 1, ones, count + zeros))
        ones, zeros = ones + flags[b], zeros + (1 - flags[b])
    sums_ref[...] = jnp.zeros_like(sums_ref)
    row_ids = lax.broadcasted_iota(jnp.int32, (META, size), 0)
    meta = jnp.zeros((META, size), jnp.float32)
    for s in range(SLOTS):
        place = sum(jnp.where(slots[b] == s, b, 0) for b in range(blocks))
        row = pl.multiple_of(place // blk_cols * size, size)
        col = pl.multiple_of(place % blk_cols * size, size)
        block = weights_ref[pl.ds(row, size), pl.ds(col, size)]
        block = jnp.where(s < count, block, jnp.zeros_like(block))
        packet_ref[pl.ds(s * size, size), :] = block
        sums_ref[:, pl.ds(col, size)] += jnp.sum(block.astype(jnp.float32), axis=0, keepdims=True)
        meta = jnp.where(row_ids == s, place.astype(jnp.float32), meta)
    for b in range(blocks):
        kept = kept_ref[b // blk_cols, b % blk_cols].astype(jnp.float32)
        meta = jnp.where(row_ids == SLOTS + b, kept, meta)
    packet_ref[pl.ds(SLOTS * size, META), :] = meta.astype(packet_ref.dtype)


def rows_of(sums_ref):
    size = 128
    parts = [
        sums_ref[r : r + 1, at : at + size]
        for r in range(sums_ref.shape[0])
        for at in range(0, sums_ref.shape[1], size)
    ]
    return jnp.concatenate(parts, axis=0)


def split(x):
    high = x.astype(jnp.bfloat16)
    return high, (x - high.astype(jnp.float32)).astype(jnp.bfloat16)


def add_kernel(one_ref, other_ref, out_ref):
    out_ref[...] = one_ref[...] + other_ref[...]


def relay_kernel(routes, riding, sums_ref, *refs):
    packet_refs, sent_refs = refs[: -len(routes)], refs[-len(routes) :]
    rows = packet_refs[0].shape[0]
    if riding:
        high, low = split(rows_of(sums_ref))
    for sent_ref, (route, rider) in zip(sent_refs, routes):
        for at, source in enumerate(route):
            sent_ref[pl.ds(at * rows, rows), :] = packet_refs[source][...]
        if rider:
            first = len(route) * rows
            sent_ref[pl.ds(first, high.shape[0]), :] = high
            sent_ref[pl.ds(first + high.shape[0], high.shape[0]), :] = low


def spread(blk_rows, blk_cols, size, packets, right):
    my_row = lax.axis_index("gc")
    for m, packet in packets.items():
        base = (my_row ^ m) * blk_rows
        for s, place in enumerate(places_in(packet, size)):
            row = pl.multiple_of((base + place // blk_cols) * size, size)
            col = pl.multiple_of(place % blk_cols * size, size)
            right[pl.ds(row, size), pl.ds(col, size)] = packet[pl.ds(s * size, size), :]


def packets_in(refs, table, rows):
    return {m: refs[n].at[pl.ds(at * rows, rows), :] for m, (n, at) in table.items()}


def spread_kernel(blk_rows, blk_cols, right_at, *refs):
    *refs, right, left = refs
    rows, size = refs[0].shape
    right[...] = jnp.zeros_like(right)
    left[...] = jnp.zeros_like(left)
    spread(blk_rows, blk_cols, size, packets_in(refs, right_at, rows), right)


def expand_kernel(right_at, riders, evens, blk_cols, sums_ref, *refs):
    *pairs, _, _, inflated_ref, total_ref, right, left = refs[: len(evens)] + refs[-6:]
    refs = refs[len(evens) : -6]
    rows, size = refs[0].shape
    blk_rows = inflated_ref.shape[0] // size
    spread(blk_rows, blk_cols, size, packets_in(refs, right_at, rows), right)
    sums = rows_of(sums_ref)
    for n, at in riders:
        high = refs[n][pl.ds(at * rows, sums.shape[0]), :].astype(jnp.float32)
        low = refs[n][pl.ds(at * rows + sums.shape[0], sums.shape[0]), :].astype(jnp.float32)
        sums = sums + (high + low)
    inverse = 1.0 / sums
    my_col = lax.axis_index("gr")
    for n in range(2 * len(evens)):
        gr = my_col // 2 * 2 + n % 2 ^ evens[n // 2]
        scales = []
        for j in range(blk_cols):
            scale = inverse[j : j + 1]
            for r in range(1, 2 * len(evens)):
                scale = jnp.where(gr == r, inverse[r * blk_cols + j : r * blk_cols + j + 1], scale)
            scales.append(scale)
        for part in range(2):
            packet = pairs[n // 2].at[pl.ds((n % 2 * 2 + part) * rows, rows), :]
            for s, place in enumerate(places_in(packet, size)):
                row = pl.multiple_of((part * blk_rows + place // blk_cols) * size, size)
                col = place % blk_cols
                scale = scales[0]
                for j in range(1, blk_cols):
                    scale = jnp.where(col == j, scales[j], scale)
                block = packet[pl.ds(s * size, size), :].astype(jnp.float32) * scale
                at = pl.multiple_of((gr * blk_cols + col) * size, size)
                left[pl.ds(row, size), pl.ds(at, size)] = block.astype(left.dtype)
    product = jnp.dot(left[...], right[...], preferred_element_type=jnp.float32)
    first = SLOTS * size
    flags = [ref[pl.ds(first, META), :].astype(jnp.float32) for ref in (refs[0], refs[1])]
    for j in range(blk_cols):
        at = slice(j * size, (j + 1) * size)
        own = inverse[j : j + 1]
        for r in range(1, 2 * len(evens)):
            own = jnp.where(my_col == r, inverse[r * blk_cols + j : r * blk_cols + j + 1], own)
        total = jnp.zeros((1, size), jnp.float32)
        for i in range(2 * blk_rows):
            part, flag = i // blk_rows, SLOTS + i % blk_rows * blk_cols + j
            kept = product[i * size : (i + 1) * size, at] * own
            kept = kept * flags[part][flag : flag + 1]
            squared = kept * kept
            if part == 0:
                inflated_ref[i * size : (i + 1) * size, at] = squared
            total = total + jnp.sum(squared, axis=0, keepdims=True)
        total_ref[:, at] = total


def shards(weights, in_pattern, out_pattern):
    blk_rows, blk_cols = in_pattern.shape
    local_rows, local_cols = weights.shape
    size = local_rows // blk_rows
    gr_size, gc_size = lax.axis_size("gr"), lax.axis_size("gc")
    order_size = local_rows * gc_size
    sums_shape = jax.ShapeDtypeStruct((1, local_cols), jnp.float32)
    rows = SLOTS * size + META
    packet, sums = pl.pallas_call(
        pack_kernel,
        out_shape=(jax.ShapeDtypeStruct((rows, size), weights.dtype), sums_shape),
        in_specs=[HBM] * 3,
        out_specs=(VMEM, VMEM),
        scratch_shapes=[
            pltpu.SMEM(in_pattern.shape, in_pattern.dtype),
            pltpu.SMEM(out_pattern.shape, out_pattern.dtype),
            pltpu.VMEM(weights.shape, weights.dtype),
            pltpu.SemaphoreType.DMA((3,)),
        ],
        compiler_params=PARAMS,
        name="pack",
    )(in_hbm(in_pattern), in_hbm(out_pattern), in_hbm(weights))

    arrays, right_at = [packet], {0: (0, 0)}

    def keep(array, masks):
        arrays.append(array)
        right_at.update({m: (len(arrays) - 1, at) for at, m in enumerate(masks)})

    riding = gc_size == 8
    if riding:
        sums = pl.pallas_call(
            add_kernel,
            out_shape=sums_shape,
            in_specs=[VMEM] * 2,
            out_specs=VMEM,
            compiler_params=PARAMS,
            cost_estimate=LONG,
            name="add",
        )(sums, swap(sums, "gc", 5))
    else:
        sums = lax.psum(sums, "gc")
    for bit in reversed(bits_of(gc_size)):
        keep(swap(packet, "gc", bit), [bit])
    sums = lax.all_gather(sums, "gr", tiled=True)

    hops = {}
    for mask in range(gc_size):
        if mask not in right_at and min(mask.bit_count(), max(2, gc_size.bit_length() - 2)) == 2:
            parent, hop = way_to(mask, "gc")
            hops.setdefault(hop, []).append((mask, parent))
    routes = [([right_at[parent][0] for _, parent in hop], riding) for hop in hops.values()]
    routes.append(([0, right_at[1][0]], False))
    extra = 2 * gr_size * blk_cols
    sent = pl.pallas_call(
        functools.partial(relay_kernel, routes, riding),
        out_shape=[
            jax.ShapeDtypeStruct((len(route) * rows + extra * rider, size), packet.dtype)
            for route, rider in routes
        ],
        in_specs=[VMEM] * (1 + len(arrays)),
        out_specs=[VMEM] * len(routes),
        compiler_params=PARAMS,
        name="relay",
    )(sums, *arrays)
    cores = [[i, i + 1] for i in range(0, gr_size, 2)]
    pairs = {0: sent[-1]}
    for bit in bits_of(gr_size)[:-1]:
        pairs.update({m | bit: swap(pair, "gr", bit) for m, pair in list(pairs.items())})
    lefts = [
        lax.all_gather(pair, "gr", axis_index_groups=cores, tiled=True) for pair in pairs.values()
    ]
    right, left = pl.pallas_call(
        functools.partial(spread_kernel, blk_rows, blk_cols, dict(right_at)),
        out_shape=(
            jax.ShapeDtypeStruct((order_size, local_cols), weights.dtype),
            jax.ShapeDtypeStruct((2 * local_rows, order_size), weights.dtype),
        ),
        in_specs=[VMEM] * len(arrays),
        out_specs=(VMEM, VMEM),
        compiler_params=PARAMS,
        name="spread",
    )(*arrays)
    early, riders = set(right_at), []
    for (hop, masks), buffer in zip(hops.items(), sent):
        keep(swap(buffer, "gc", hop), [m for m, _ in masks])
        if riding:
            riders.append((len(arrays) - 1, len(masks)))
    for mask in sorted(set(range(gc_size)) - set(right_at), key=lambda m: m.bit_count()):
        parent, hop = way_to(mask, "gc")
        n, at = right_at[parent]
        keep(swap(arrays[n][at * rows : (at + 1) * rows], "gc", hop), [mask])
    late_at = {m: at for m, at in right_at.items() if m not in early}
    inflated, sums, *_ = pl.pallas_call(
        functools.partial(expand_kernel, late_at, riders, list(pairs), blk_cols),
        out_shape=(jax.ShapeDtypeStruct(weights.shape, jnp.float32), sums_shape, right, left),
        in_specs=[VMEM] * (3 + len(lefts) + len(arrays)),
        out_specs=[VMEM] * 4,
        input_output_aliases={1 + len(lefts) + len(arrays): 2, 2 + len(lefts) + len(arrays): 3},
        compiler_params=PARAMS,
        name="expand",
    )(sums, *lefts, *arrays, right, left)
    output_total = sums
    for mask in range(2, gc_size, 2):
        output_total = output_total + swap(sums, "gc", mask)
    return (inflated / output_total * float(order_size)).astype(jnp.bfloat16)


def solution(mesh):
    in_specs = (P("gc", "gr"), P("gc", "gr"), P("gc", "gr"))
    out_specs = P("gc", "gr")
    return jax.shard_map(shards, mesh=mesh, in_specs=in_specs, out_specs=out_specs, check_vma=False)
```

```python
import functools

import jax
import jax.numpy as jnp
from jax import lax
from jax.experimental import pallas as pl
from jax.experimental.pallas import tpu as pltpu
from jax.sharding import PartitionSpec as P

SLOTS = 4
META = 16
VMEM = pl.BlockSpec(memory_space=pltpu.VMEM)
HBM = pl.BlockSpec(memory_space=pltpu.HBM)
PARAMS = pltpu.CompilerParams(vmem_limit_bytes=16 << 20)
LONG = pl.CostEstimate(flops=10**10, bytes_accessed=0, transcendentals=0)


def in_hbm(x):
    return pltpu.with_memory_space_constraint(x, pltpu.HBM)


def bits_of(size):
    return [1 << b for b in reversed(range(size.bit_length() - 1))]


def swap(x, axis, mask):
    return lax.ppermute(x, axis, [(i, i ^ mask) for i in range(lax.axis_size(axis))])


def way_to(mask, axis):
    full = lax.axis_size(axis) - 1
    if mask == full and mask.bit_count() > 2:
        return 1, mask ^ 1
    bits = [bit for bit in bits_of(full + 1) if mask & bit]
    last = bits[min(1, len(bits) - 1)]
    return mask ^ last, last


def places_in(packet, size):
    meta = packet[pl.ds(SLOTS * size, META), :].astype(jnp.float32)
    return [jnp.max(meta[s : s + 1, :]).astype(jnp.int32) for s in range(SLOTS)]


def pack_kernel(flags_hbm, kept_hbm, weights_hbm, packet_ref, sums_ref, flags_ref, kept_ref, weights_ref, sems):
    copies = [
        pltpu.make_async_copy(flags_hbm, flags_ref, sems.at[0]),
        pltpu.make_async_copy(kept_hbm, kept_ref, sems.at[1]),
        pltpu.make_async_copy(weights_hbm, weights_ref, sems.at[2]),
    ]
    for copy in copies:
        copy.start()
    for copy in copies:
        copy.wait()
    blk_rows, blk_cols = flags_ref.shape
    size = weights_ref.shape[0] // blk_rows
    blocks = blk_rows * blk_cols
    flags = [flags_ref[b // blk_cols, b % blk_cols] for b in range(blocks)]
    count = sum(flags)
    ones, zeros, slots = 0, 0, []
    for b in range(blocks):
        slots.append(jnp.where(flags[b] == 1, ones, count + zeros))
        ones, zeros = ones + flags[b], zeros + (1 - flags[b])
    sums_ref[...] = jnp.zeros_like(sums_ref)
    row_ids = lax.broadcasted_iota(jnp.int32, (META, size), 0)
    meta = jnp.zeros((META, size), jnp.float32)
    for s in range(SLOTS):
        place = sum(jnp.where(slots[b] == s, b, 0) for b in range(blocks))
        row = pl.multiple_of(place // blk_cols * size, size)
        col = pl.multiple_of(place % blk_cols * size, size)
        block = weights_ref[pl.ds(row, size), pl.ds(col, size)]
        block = jnp.where(s < count, block, jnp.zeros_like(block))
        packet_ref[pl.ds(s * size, size), :] = block
        sums_ref[:, pl.ds(col, size)] += jnp.sum(block.astype(jnp.float32), axis=0, keepdims=True)
        meta = jnp.where(row_ids == s, place.astype(jnp.float32), meta)
    for b in range(blocks):
        kept = kept_ref[b // blk_cols, b % blk_cols].astype(jnp.float32)
        meta = jnp.where(row_ids == SLOTS + b, kept, meta)
    packet_ref[pl.ds(SLOTS * size, META), :] = meta.astype(packet_ref.dtype)


def rows_of(sums_ref):
    size = 128
    parts = [
        sums_ref[r : r + 1, at : at + size]
        for r in range(sums_ref.shape[0])
        for at in range(0, sums_ref.shape[1], size)
    ]
    return jnp.concatenate(parts, axis=0)


def split(x):
    high = x.astype(jnp.bfloat16)
    return high, (x - high.astype(jnp.float32)).astype(jnp.bfloat16)


def add_kernel(one_ref, other_ref, out_ref):
    out_ref[...] = one_ref[...] + other_ref[...]


def relay_kernel(routes, riding, sums_ref, *refs):
    packet_refs, sent_refs = refs[: -len(routes)], refs[-len(routes) :]
    rows = packet_refs[0].shape[0]
    if riding:
        high, low = split(rows_of(sums_ref))
    for sent_ref, (route, rider) in zip(sent_refs, routes):
        for at, source in enumerate(route):
            sent_ref[pl.ds(at * rows, rows), :] = packet_refs[source][...]
        if rider:
            first = len(route) * rows
            sent_ref[pl.ds(first, high.shape[0]), :] = high
            sent_ref[pl.ds(first + high.shape[0], high.shape[0]), :] = low


def spread(blk_rows, blk_cols, size, packets, right):
    my_row = lax.axis_index("gc")
    for m, packet in packets.items():
        base = (my_row ^ m) * blk_rows
        for s, place in enumerate(places_in(packet, size)):
            row = pl.multiple_of((base + place // blk_cols) * size, size)
            col = pl.multiple_of(place % blk_cols * size, size)
            right[pl.ds(row, size), pl.ds(col, size)] = packet[pl.ds(s * size, size), :]


def packets_in(refs, table, rows):
    return {m: refs[n].at[pl.ds(at * rows, rows), :] for m, (n, at) in table.items()}


def spread_kernel(blk_rows, blk_cols, right_at, *refs):
    *refs, right, left = refs
    rows, size = refs[0].shape
    right[...] = jnp.zeros_like(right)
    left[...] = jnp.zeros_like(left)
    spread(blk_rows, blk_cols, size, packets_in(refs, right_at, rows), right)


def expand_kernel(right_at, riders, evens, blk_cols, sums_ref, *refs):
    *pairs, _, _, inflated_ref, total_ref, right, left = refs[: len(evens)] + refs[-6:]
    refs = refs[len(evens) : -6]
    rows, size = refs[0].shape
    blk_rows = inflated_ref.shape[0] // size
    spread(blk_rows, blk_cols, size, packets_in(refs, right_at, rows), right)
    sums = rows_of(sums_ref)
    for n, at in riders:
        high = refs[n][pl.ds(at * rows, sums.shape[0]), :].astype(jnp.float32)
        low = refs[n][pl.ds(at * rows + sums.shape[0], sums.shape[0]), :].astype(jnp.float32)
        sums = sums + (high + low)
    inverse = 1.0 / sums
    my_col = lax.axis_index("gr")
    for n in range(2 * len(evens)):
        gr = my_col // 2 * 2 + n % 2 ^ evens[n // 2]
        scales = []
        for j in range(blk_cols):
            scale = inverse[j : j + 1]
            for m in range(1, 2 * len(evens)):
                there = inverse[m * blk_cols + j : m * blk_cols + j + 1]
                scale = jnp.where(my_col ^ m == gr, there, scale)
            scales.append(scale)
        for part in range(2):
            packet = pairs[n // 2].at[pl.ds((n % 2 * 2 + part) * rows, rows), :]
            for s, place in enumerate(places_in(packet, size)):
                row = pl.multiple_of((part * blk_rows + place // blk_cols) * size, size)
                col = place % blk_cols
                scale = scales[0]
                for j in range(1, blk_cols):
                    scale = jnp.where(col == j, scales[j], scale)
                block = packet[pl.ds(s * size, size), :].astype(jnp.float32) * scale
                at = pl.multiple_of((gr * blk_cols + col) * size, size)
                left[pl.ds(row, size), pl.ds(at, size)] = block.astype(left.dtype)
    product = jnp.dot(left[...], right[...], preferred_element_type=jnp.float32)
    first = SLOTS * size
    flags = [ref[pl.ds(first, META), :].astype(jnp.float32) for ref in (refs[0], refs[1])]
    for j in range(blk_cols):
        at = slice(j * size, (j + 1) * size)
        own = inverse[j : j + 1]
        total = jnp.zeros((1, size), jnp.float32)
        for i in range(2 * blk_rows):
            part, flag = i // blk_rows, SLOTS + i % blk_rows * blk_cols + j
            kept = product[i * size : (i + 1) * size, at] * own
            kept = kept * flags[part][flag : flag + 1]
            squared = kept * kept
            if part == 0:
                inflated_ref[i * size : (i + 1) * size, at] = squared
            total = total + jnp.sum(squared, axis=0, keepdims=True)
        total_ref[:, at] = total


def shards(weights, in_pattern, out_pattern):
    blk_rows, blk_cols = in_pattern.shape
    local_rows, local_cols = weights.shape
    size = local_rows // blk_rows
    gr_size, gc_size = lax.axis_size("gr"), lax.axis_size("gc")
    order_size = local_rows * gc_size
    sums_shape = jax.ShapeDtypeStruct((1, local_cols), jnp.float32)
    rows = SLOTS * size + META
    packet, sums = pl.pallas_call(
        pack_kernel,
        out_shape=(jax.ShapeDtypeStruct((rows, size), weights.dtype), sums_shape),
        in_specs=[HBM] * 3,
        out_specs=(VMEM, VMEM),
        scratch_shapes=[
            pltpu.SMEM(in_pattern.shape, in_pattern.dtype),
            pltpu.SMEM(out_pattern.shape, out_pattern.dtype),
            pltpu.VMEM(weights.shape, weights.dtype),
            pltpu.SemaphoreType.DMA((3,)),
        ],
        compiler_params=PARAMS,
        name="pack",
    )(in_hbm(in_pattern), in_hbm(out_pattern), in_hbm(weights))

    arrays, right_at = [packet], {0: (0, 0)}

    def keep(array, masks):
        arrays.append(array)
        right_at.update({m: (len(arrays) - 1, at) for at, m in enumerate(masks)})

    riding = gc_size == 8
    if riding:
        sums = pl.pallas_call(
            add_kernel,
            out_shape=jax.ShapeDtypeStruct(sums.shape, sums.dtype),
            in_specs=[VMEM] * 2,
            out_specs=VMEM,
            compiler_params=PARAMS,
            cost_estimate=LONG,
            name="add",
        )(sums, swap(sums, "gc", 5))
    else:
        sums = lax.psum(sums, "gc")
    for bit in reversed(bits_of(gc_size)):
        keep(swap(packet, "gc", bit), [bit])
    sums = jnp.concatenate([sums] + [swap(sums, "gr", m) for m in range(1, gr_size)], axis=0)

    hops = {}
    for mask in range(gc_size):
        if mask not in right_at and min(mask.bit_count(), max(2, gc_size.bit_length() - 2)) == 2:
            parent, hop = way_to(mask, "gc")
            hops.setdefault(hop, []).append((mask, parent))
    routes = [([right_at[parent][0] for _, parent in hop], riding) for hop in hops.values()]
    routes.append(([0, right_at[1][0]], False))
    extra = 2 * gr_size * blk_cols
    sent = pl.pallas_call(
        functools.partial(relay_kernel, routes, riding),
        out_shape=[
            jax.ShapeDtypeStruct((len(route) * rows + extra * rider, size), packet.dtype)
            for route, rider in routes
        ],
        in_specs=[VMEM] * (1 + len(arrays)),
        out_specs=[VMEM] * len(routes),
        compiler_params=PARAMS,
        name="relay",
    )(sums, *arrays)
    cores = [[i, i + 1] for i in range(0, gr_size, 2)]
    pairs = {0: sent[-1]}
    for bit in bits_of(gr_size)[:-1]:
        pairs.update({m | bit: swap(pair, "gr", bit) for m, pair in list(pairs.items())})
    lefts = [
        lax.all_gather(pair, "gr", axis_index_groups=cores, tiled=True) for pair in pairs.values()
    ]
    right, left = pl.pallas_call(
        functools.partial(spread_kernel, blk_rows, blk_cols, dict(right_at)),
        out_shape=(
            jax.ShapeDtypeStruct((order_size, local_cols), weights.dtype),
            jax.ShapeDtypeStruct((2 * local_rows, order_size), weights.dtype),
        ),
        in_specs=[VMEM] * len(arrays),
        out_specs=(VMEM, VMEM),
        compiler_params=PARAMS,
        name="spread",
    )(*arrays)
    early, riders = set(right_at), []
    for (hop, masks), buffer in zip(hops.items(), sent):
        keep(swap(buffer, "gc", hop), [m for m, _ in masks])
        if riding:
            riders.append((len(arrays) - 1, len(masks)))
    for mask in sorted(set(range(gc_size)) - set(right_at), key=lambda m: m.bit_count()):
        parent, hop = way_to(mask, "gc")
        n, at = right_at[parent]
        keep(swap(arrays[n][at * rows : (at + 1) * rows], "gc", hop), [mask])
    late_at = {m: at for m, at in right_at.items() if m not in early}
    inflated, sums, *_ = pl.pallas_call(
        functools.partial(expand_kernel, late_at, riders, list(pairs), blk_cols),
        out_shape=(jax.ShapeDtypeStruct(weights.shape, jnp.float32), sums_shape, right, left),
        in_specs=[VMEM] * (3 + len(lefts) + len(arrays)),
        out_specs=[VMEM] * 4,
        input_output_aliases={1 + len(lefts) + len(arrays): 2, 2 + len(lefts) + len(arrays): 3},
        compiler_params=PARAMS,
        name="expand",
    )(sums, *lefts, *arrays, right, left)
    output_total = sums
    for mask in range(2, gc_size, 2):
        output_total = output_total + swap(sums, "gc", mask)
    return (inflated / output_total * float(order_size)).astype(jnp.bfloat16)


def solution(mesh):
    in_specs = (P("gc", "gr"), P("gc", "gr"), P("gc", "gr"))
    out_specs = P("gc", "gr")
    return jax.shard_map(shards, mesh=mesh, in_specs=in_specs, out_specs=out_specs, check_vma=False)
```

```python
import functools

import jax
import jax.numpy as jnp
from jax import lax
from jax.experimental import pallas as pl
from jax.experimental.pallas import tpu as pltpu
from jax.sharding import PartitionSpec as P

SLOTS = 4
META = 16
VMEM = pl.BlockSpec(memory_space=pltpu.VMEM)
HBM = pl.BlockSpec(memory_space=pltpu.HBM)
PARAMS = pltpu.CompilerParams(vmem_limit_bytes=16 << 20)
LONG = pl.CostEstimate(flops=10**10, bytes_accessed=0, transcendentals=0)


def in_hbm(x):
    return pltpu.with_memory_space_constraint(x, pltpu.HBM)


def bits_of(size):
    return [1 << b for b in reversed(range(size.bit_length() - 1))]


def swap(x, axis, mask):
    return lax.ppermute(x, axis, [(i, i ^ mask) for i in range(lax.axis_size(axis))])


def way_to(mask, axis):
    full = lax.axis_size(axis) - 1
    if mask == full and mask.bit_count() > 2:
        return 1, mask ^ 1
    bits = [bit for bit in bits_of(full + 1) if mask & bit]
    last = bits[min(1, len(bits) - 1)]
    return mask ^ last, last


def places_in(packet, size):
    meta = packet[pl.ds(SLOTS * size, META), :].astype(jnp.float32)
    meta = meta.astype(jnp.int32)
    return [meta[s, 0] for s in range(SLOTS)]


def pack_kernel(flags_hbm, kept_hbm, weights_hbm, packet_ref, sums_ref, flags_ref, kept_ref, weights_ref, sems):
    copies = [
        pltpu.make_async_copy(flags_hbm, flags_ref, sems.at[0]),
        pltpu.make_async_copy(kept_hbm, kept_ref, sems.at[1]),
        pltpu.make_async_copy(weights_hbm, weights_ref, sems.at[2]),
    ]
    for copy in copies:
        copy.start()
    for copy in copies:
        copy.wait()
    blk_rows, blk_cols = flags_ref.shape
    size = weights_ref.shape[0] // blk_rows
    blocks = blk_rows * blk_cols
    flags = [flags_ref[b // blk_cols, b % blk_cols] for b in range(blocks)]
    count = sum(flags)
    ones, zeros, slots = 0, 0, []
    for b in range(blocks):
        slots.append(jnp.where(flags[b] == 1, ones, count + zeros))
        ones, zeros = ones + flags[b], zeros + (1 - flags[b])
    sums_ref[...] = jnp.zeros_like(sums_ref)
    row_ids = lax.broadcasted_iota(jnp.int32, (META, size), 0)
    meta = jnp.zeros((META, size), jnp.float32)
    for s in range(SLOTS):
        place = sum(jnp.where(slots[b] == s, b, 0) for b in range(blocks))
        row = pl.multiple_of(place // blk_cols * size, size)
        col = pl.multiple_of(place % blk_cols * size, size)
        block = weights_ref[pl.ds(row, size), pl.ds(col, size)]
        block = jnp.where(s < count, block, jnp.zeros_like(block))
        packet_ref[pl.ds(s * size, size), :] = block
        sums_ref[:, pl.ds(col, size)] += jnp.sum(block.astype(jnp.float32), axis=0, keepdims=True)
        meta = jnp.where(row_ids == s, place.astype(jnp.float32), meta)
    for b in range(blocks):
        kept = kept_ref[b // blk_cols, b % blk_cols].astype(jnp.float32)
        meta = jnp.where(row_ids == SLOTS + b, kept, meta)
    packet_ref[pl.ds(SLOTS * size, META), :] = meta.astype(packet_ref.dtype)


def rows_of(sums_ref):
    size = 128
    parts = [
        sums_ref[r : r + 1, at : at + size]
        for r in range(sums_ref.shape[0])
        for at in range(0, sums_ref.shape[1], size)
    ]
    return jnp.concatenate(parts, axis=0)


def split(x):
    high = x.astype(jnp.bfloat16)
    return high, (x - high.astype(jnp.float32)).astype(jnp.bfloat16)


def add_kernel(one_ref, other_ref, out_ref):
    out_ref[...] = one_ref[...] + other_ref[...]


def relay_kernel(routes, riding, sums_ref, *refs):
    packet_refs, sent_refs = refs[: -len(routes)], refs[-len(routes) :]
    rows = packet_refs[0].shape[0]
    if riding:
        high, low = split(rows_of(sums_ref))
    for sent_ref, (route, rider) in zip(sent_refs, routes):
        for at, source in enumerate(route):
            sent_ref[pl.ds(at * rows, rows), :] = packet_refs[source][...]
        if rider:
            first = len(route) * rows
            sent_ref[pl.ds(first, high.shape[0]), :] = high
            sent_ref[pl.ds(first + high.shape[0], high.shape[0]), :] = low


def spread(blk_rows, blk_cols, size, packets, right):
    my_row = lax.axis_index("gc")
    for m, packet in packets.items():
        base = (my_row ^ m) * blk_rows
        for s, place in enumerate(places_in(packet, size)):
            row = pl.multiple_of((base + place // blk_cols) * size, size)
            col = pl.multiple_of(place % blk_cols * size, size)
            right[pl.ds(row, size), pl.ds(col, size)] = packet[pl.ds(s * size, size), :]


def packets_in(refs, table, rows):
    return {m: refs[n].at[pl.ds(at * rows, rows), :] for m, (n, at) in table.items()}


def spread_kernel(blk_rows, blk_cols, right_at, *refs):
    *refs, right, left = refs
    rows, size = refs[0].shape
    right[...] = jnp.zeros_like(right)
    left[...] = jnp.zeros_like(left)
    spread(blk_rows, blk_cols, size, packets_in(refs, right_at, rows), right)


def expand_kernel(right_at, riders, evens, blk_cols, sums_ref, *refs):
    *pairs, _, _, inflated_ref, total_ref, right, left = refs[: len(evens)] + refs[-6:]
    refs = refs[len(evens) : -6]
    rows, size = refs[0].shape
    blk_rows = inflated_ref.shape[0] // size
    spread(blk_rows, blk_cols, size, packets_in(refs, right_at, rows), right)
    sums = rows_of(sums_ref)
    for n, at in riders:
        high = refs[n][pl.ds(at * rows, sums.shape[0]), :].astype(jnp.float32)
        low = refs[n][pl.ds(at * rows + sums.shape[0], sums.shape[0]), :].astype(jnp.float32)
        sums = sums + (high + low)
    inverse = 1.0 / sums
    my_col = lax.axis_index("gr")
    for n in range(2 * len(evens)):
        gr = my_col // 2 * 2 + n % 2 ^ evens[n // 2]
        scales = []
        for j in range(blk_cols):
            scale = inverse[j : j + 1]
            for m in range(1, 2 * len(evens)):
                there = inverse[m * blk_cols + j : m * blk_cols + j + 1]
                scale = jnp.where(my_col ^ m == gr, there, scale)
            scales.append(scale)
        for part in range(2):
            packet = pairs[n // 2].at[pl.ds((n % 2 * 2 + part) * rows, rows), :]
            for s, place in enumerate(places_in(packet, size)):
                row = pl.multiple_of((part * blk_rows + place // blk_cols) * size, size)
                col = place % blk_cols
                scale = scales[0]
                for j in range(1, blk_cols):
                    scale = jnp.where(col == j, scales[j], scale)
                block = packet[pl.ds(s * size, size), :].astype(jnp.float32) * scale
                at = pl.multiple_of((gr * blk_cols + col) * size, size)
                left[pl.ds(row, size), pl.ds(at, size)] = block.astype(left.dtype)
    product = jnp.dot(left[...], right[...], preferred_element_type=jnp.float32)
    first = SLOTS * size
    flags = [ref[pl.ds(first, META), :].astype(jnp.float32) for ref in (refs[0], refs[1])]
    for j in range(blk_cols):
        at = slice(j * size, (j + 1) * size)
        own = inverse[j : j + 1]
        total = jnp.zeros((1, size), jnp.float32)
        for i in range(2 * blk_rows):
            part, flag = i // blk_rows, SLOTS + i % blk_rows * blk_cols + j
            kept = product[i * size : (i + 1) * size, at] * own
            kept = kept * flags[part][flag : flag + 1]
            squared = kept * kept
            if part == 0:
                inflated_ref[i * size : (i + 1) * size, at] = squared
            total = total + jnp.sum(squared, axis=0, keepdims=True)
        total_ref[:, at] = total


def shards(weights, in_pattern, out_pattern):
    blk_rows, blk_cols = in_pattern.shape
    local_rows, local_cols = weights.shape
    size = local_rows // blk_rows
    gr_size, gc_size = lax.axis_size("gr"), lax.axis_size("gc")
    order_size = local_rows * gc_size
    sums_shape = jax.ShapeDtypeStruct((1, local_cols), jnp.float32)
    rows = SLOTS * size + META
    packet, sums = pl.pallas_call(
        pack_kernel,
        out_shape=(jax.ShapeDtypeStruct((rows, size), weights.dtype), sums_shape),
        in_specs=[HBM] * 3,
        out_specs=(VMEM, VMEM),
        scratch_shapes=[
            pltpu.SMEM(in_pattern.shape, in_pattern.dtype),
            pltpu.SMEM(out_pattern.shape, out_pattern.dtype),
            pltpu.VMEM(weights.shape, weights.dtype),
            pltpu.SemaphoreType.DMA((3,)),
        ],
        compiler_params=PARAMS,
        name="pack",
    )(in_hbm(in_pattern), in_hbm(out_pattern), in_hbm(weights))

    arrays, right_at = [packet], {0: (0, 0)}

    def keep(array, masks):
        arrays.append(array)
        right_at.update({m: (len(arrays) - 1, at) for at, m in enumerate(masks)})

    riding = gc_size == 8
    if riding:
        sums = pl.pallas_call(
            add_kernel,
            out_shape=jax.ShapeDtypeStruct(sums.shape, sums.dtype),
            in_specs=[VMEM] * 2,
            out_specs=VMEM,
            compiler_params=PARAMS,
            cost_estimate=LONG,
            name="add",
        )(sums, swap(sums, "gc", 5))
    else:
        sums = lax.psum(sums, "gc")
    for bit in reversed(bits_of(gc_size)):
        keep(swap(packet, "gc", bit), [bit])
    sums = jnp.concatenate([sums] + [swap(sums, "gr", m) for m in range(1, gr_size)], axis=0)

    hops = {}
    for mask in range(gc_size):
        if mask not in right_at and min(mask.bit_count(), max(2, gc_size.bit_length() - 2)) == 2:
            parent, hop = way_to(mask, "gc")
            hops.setdefault(hop, []).append((mask, parent))
    routes = [([right_at[parent][0] for _, parent in hop], riding) for hop in hops.values()]
    routes.append(([0, right_at[1][0]], False))
    extra = 2 * gr_size * blk_cols
    sent = pl.pallas_call(
        functools.partial(relay_kernel, routes, riding),
        out_shape=[
            jax.ShapeDtypeStruct((len(route) * rows + extra * rider, size), packet.dtype)
            for route, rider in routes
        ],
        in_specs=[VMEM] * (1 + len(arrays)),
        out_specs=[VMEM] * len(routes),
        compiler_params=PARAMS,
        name="relay",
    )(sums, *arrays)
    cores = [[i, i + 1] for i in range(0, gr_size, 2)]
    pairs = {0: sent[-1]}
    for bit in bits_of(gr_size)[:-1]:
        pairs.update({m | bit: swap(pair, "gr", bit) for m, pair in list(pairs.items())})
    lefts = [
        lax.all_gather(pair, "gr", axis_index_groups=cores, tiled=True) for pair in pairs.values()
    ]
    right, left = pl.pallas_call(
        functools.partial(spread_kernel, blk_rows, blk_cols, dict(right_at)),
        out_shape=(
            jax.ShapeDtypeStruct((order_size, local_cols), weights.dtype),
            jax.ShapeDtypeStruct((2 * local_rows, order_size), weights.dtype),
        ),
        in_specs=[VMEM] * len(arrays),
        out_specs=(VMEM, VMEM),
        compiler_params=PARAMS,
        name="spread",
    )(*arrays)
    early, riders = set(right_at), []
    for (hop, masks), buffer in zip(hops.items(), sent):
        keep(swap(buffer, "gc", hop), [m for m, _ in masks])
        if riding:
            riders.append((len(arrays) - 1, len(masks)))
    for mask in sorted(set(range(gc_size)) - set(right_at), key=lambda m: m.bit_count()):
        parent, hop = way_to(mask, "gc")
        n, at = right_at[parent]
        keep(swap(arrays[n][at * rows : (at + 1) * rows], "gc", hop), [mask])
    late_at = {m: at for m, at in right_at.items() if m not in early}
    inflated, sums, *_ = pl.pallas_call(
        functools.partial(expand_kernel, late_at, riders, list(pairs), blk_cols),
        out_shape=(jax.ShapeDtypeStruct(weights.shape, jnp.float32), sums_shape, right, left),
        in_specs=[VMEM] * (3 + len(lefts) + len(arrays)),
        out_specs=[VMEM] * 4,
        input_output_aliases={1 + len(lefts) + len(arrays): 2, 2 + len(lefts) + len(arrays): 3},
        compiler_params=PARAMS,
        name="expand",
    )(sums, *lefts, *arrays, right, left)
    output_total = sums
    for mask in range(2, gc_size, 2):
        output_total = output_total + swap(sums, "gc", mask)
    return (inflated / output_total * float(order_size)).astype(jnp.bfloat16)


def solution(mesh):
    in_specs = (P("gc", "gr"), P("gc", "gr"), P("gc", "gr"))
    out_specs = P("gc", "gr")
    return jax.shard_map(shards, mesh=mesh, in_specs=in_specs, out_specs=out_specs, check_vma=False)
```

```python
import functools

import jax
import jax.numpy as jnp
from jax import lax
from jax.experimental import pallas as pl
from jax.experimental.pallas import tpu as pltpu
from jax.sharding import PartitionSpec as P

SLOTS = 4
META = 16
CHUNKS = 2
VMEM = pl.BlockSpec(memory_space=pltpu.VMEM)
HBM = pl.BlockSpec(memory_space=pltpu.HBM)
PARAMS = pltpu.CompilerParams(vmem_limit_bytes=16 << 20)
LONG = pl.CostEstimate(flops=10**10, bytes_accessed=0, transcendentals=0)


def in_hbm(x):
    return pltpu.with_memory_space_constraint(x, pltpu.HBM)


def bits_of(size):
    return [1 << b for b in reversed(range(size.bit_length() - 1))]


def swap(x, axis, mask):
    return lax.ppermute(x, axis, [(i, i ^ mask) for i in range(lax.axis_size(axis))])


def way_to(mask, axis):
    full = lax.axis_size(axis) - 1
    if mask == full and mask.bit_count() > 2:
        return 1, mask ^ 1
    bits = [bit for bit in bits_of(full + 1) if mask & bit]
    last = bits[min(1, len(bits) - 1)]
    return mask ^ last, last


def places_in(packet, size):
    meta = packet[pl.ds(SLOTS * size, META), :].astype(jnp.float32)
    meta = meta.astype(jnp.int32)
    return [meta[s, 0] for s in range(SLOTS)]


def pack_kernel(flags_hbm, kept_hbm, weights_hbm, packet_ref, sums_ref, flags_ref, kept_ref, weights_ref, sems):
    copies = [
        pltpu.make_async_copy(flags_hbm, flags_ref, sems.at[0]),
        pltpu.make_async_copy(kept_hbm, kept_ref, sems.at[1]),
        pltpu.make_async_copy(weights_hbm, weights_ref, sems.at[2]),
    ]
    for copy in copies:
        copy.start()
    for copy in copies:
        copy.wait()
    blk_rows, blk_cols = flags_ref.shape
    size = weights_ref.shape[0] // blk_rows
    blocks = blk_rows * blk_cols
    flags = [flags_ref[b // blk_cols, b % blk_cols] for b in range(blocks)]
    count = sum(flags)
    ones, zeros, slots = 0, 0, []
    for b in range(blocks):
        slots.append(jnp.where(flags[b] == 1, ones, count + zeros))
        ones, zeros = ones + flags[b], zeros + (1 - flags[b])
    sums_ref[...] = jnp.zeros_like(sums_ref)
    row_ids = lax.broadcasted_iota(jnp.int32, (META, size), 0)
    meta = jnp.zeros((META, size), jnp.float32)
    for s in range(SLOTS):
        place = sum(jnp.where(slots[b] == s, b, 0) for b in range(blocks))
        row = pl.multiple_of(place // blk_cols * size, size)
        col = pl.multiple_of(place % blk_cols * size, size)
        block = weights_ref[pl.ds(row, size), pl.ds(col, size)]
        block = jnp.where(s < count, block, jnp.zeros_like(block))
        packet_ref[pl.ds(s * size, size), :] = block
        sums_ref[:, pl.ds(col, size)] += jnp.sum(block.astype(jnp.float32), axis=0, keepdims=True)
        meta = jnp.where(row_ids == s, place.astype(jnp.float32), meta)
    for b in range(blocks):
        kept = kept_ref[b // blk_cols, b % blk_cols].astype(jnp.float32)
        meta = jnp.where(row_ids == SLOTS + b, kept, meta)
    packet_ref[pl.ds(SLOTS * size, META), :] = meta.astype(packet_ref.dtype)


def rows_of(sums_ref):
    size = 128
    parts = [
        sums_ref[r : r + 1, at : at + size]
        for r in range(sums_ref.shape[0])
        for at in range(0, sums_ref.shape[1], size)
    ]
    return jnp.concatenate(parts, axis=0)


def split(x):
    high = x.astype(jnp.bfloat16)
    return high, (x - high.astype(jnp.float32)).astype(jnp.bfloat16)


def add_kernel(one_ref, other_ref, out_ref):
    out_ref[...] = one_ref[...] + other_ref[...]


def relay_kernel(routes, riding, sums_ref, *refs):
    packet_refs, sent_refs = refs[: -len(routes)], refs[-len(routes) :]
    rows = packet_refs[0].shape[0]
    if riding:
        high, low = split(rows_of(sums_ref))
    for sent_ref, (route, rider) in zip(sent_refs, routes):
        for at, source in enumerate(route):
            sent_ref[pl.ds(at * rows, rows), :] = packet_refs[source][...]
        if rider:
            first = len(route) * rows
            sent_ref[pl.ds(first, high.shape[0]), :] = high
            sent_ref[pl.ds(first + high.shape[0], high.shape[0]), :] = low


def spread(blk_rows, blk_cols, size, packets, right):
    my_row = lax.axis_index("gc")
    for m, packet in packets.items():
        base = (my_row ^ m) * blk_rows
        for s, place in enumerate(places_in(packet, size)):
            row = pl.multiple_of((base + place // blk_cols) * size, size)
            col = pl.multiple_of(place % blk_cols * size, size)
            right[pl.ds(row, size), pl.ds(col, size)] = packet[pl.ds(s * size, size), :]


def packets_in(refs, table, rows):
    return {m: refs[n].at[pl.ds(at * rows, rows), :] for m, (n, at) in table.items()}


def spread_kernel(blk_rows, blk_cols, right_at, *refs):
    *refs, right, left = refs
    rows, size = refs[0].shape
    right[...] = jnp.zeros_like(right)
    left[...] = jnp.zeros_like(left)
    spread(blk_rows, blk_cols, size, packets_in(refs, right_at, rows), right)


def expand_kernel(right_at, riders, evens, blk_cols, sums_ref, *refs):
    *pairs, _, _, inflated_ref, total_ref, right, left = refs[: len(evens)] + refs[-6:]
    refs = refs[len(evens) : -6]
    rows, size = refs[0].shape
    blk_rows = inflated_ref.shape[0] // size
    spread(blk_rows, blk_cols, size, packets_in(refs, right_at, rows), right)
    sums = rows_of(sums_ref)
    for n, at in riders:
        high = refs[n][pl.ds(at * rows, sums.shape[0]), :].astype(jnp.float32)
        low = refs[n][pl.ds(at * rows + sums.shape[0], sums.shape[0]), :].astype(jnp.float32)
        sums = sums + (high + low)
    inverse = 1.0 / sums
    my_col = lax.axis_index("gr")
    for n in range(2 * len(evens)):
        gr = my_col // 2 * 2 + n % 2 ^ evens[n // 2]
        scales = []
        for j in range(blk_cols):
            scale = inverse[j : j + 1]
            for m in range(1, 2 * len(evens)):
                there = inverse[m * blk_cols + j : m * blk_cols + j + 1]
                scale = jnp.where(my_col ^ m == gr, there, scale)
            scales.append(scale)
        for part in range(2):
            packet = pairs[n // 2].at[pl.ds((n % 2 * 2 + part) * rows, rows), :]
            for s, place in enumerate(places_in(packet, size)):
                row = pl.multiple_of((part * blk_rows + place // blk_cols) * size, size)
                col = place % blk_cols
                scale = scales[0]
                for j in range(1, blk_cols):
                    scale = jnp.where(col == j, scales[j], scale)
                block = packet[pl.ds(s * size, size), :].astype(jnp.float32) * scale
                at = pl.multiple_of((gr * blk_cols + col) * size, size)
                left[pl.ds(row, size), pl.ds(at, size)] = block.astype(left.dtype)
    product = jnp.dot(left[...], right[...], preferred_element_type=jnp.float32)
    first = SLOTS * size
    flags = [ref[pl.ds(first, META), :].astype(jnp.float32) for ref in (refs[0], refs[1])]
    for j in range(blk_cols):
        at = slice(j * size, (j + 1) * size)
        own = inverse[j : j + 1]
        total = jnp.zeros((1, size), jnp.float32)
        for i in range(2 * blk_rows):
            part, flag = i // blk_rows, SLOTS + i % blk_rows * blk_cols + j
            kept = product[i * size : (i + 1) * size, at] * own
            kept = kept * flags[part][flag : flag + 1]
            squared = kept * kept
            if part == 0:
                inflated_ref[i * size : (i + 1) * size, at] = squared
            total = total + jnp.sum(squared, axis=0, keepdims=True)
        total_ref[:, at] = total


def scale_kernel(order_size, inflated_ref, *refs):
    *total_refs, out_hbm, out_ref, sems = refs
    total = sum(ref[...] for ref in total_refs[1:]) + total_refs[0][...]
    scale = order_size / total
    rows = out_ref.shape[0] // CHUNKS
    copies = []
    for n in range(CHUNKS):
        at = pl.ds(n * rows, rows)
        out_ref[at, :] = (inflated_ref[at, :] * scale).astype(out_ref.dtype)
        copies.append(pltpu.make_async_copy(out_ref.at[at, :], out_hbm.at[at, :], sems.at[n]))
        copies[-1].start()
    for copy in copies:
        copy.wait()


def shards(weights, in_pattern, out_pattern):
    blk_rows, blk_cols = in_pattern.shape
    local_rows, local_cols = weights.shape
    size = local_rows // blk_rows
    gr_size, gc_size = lax.axis_size("gr"), lax.axis_size("gc")
    order_size = local_rows * gc_size
    sums_shape = jax.ShapeDtypeStruct((1, local_cols), jnp.float32)
    rows = SLOTS * size + META
    packet, sums = pl.pallas_call(
        pack_kernel,
        out_shape=(jax.ShapeDtypeStruct((rows, size), weights.dtype), sums_shape),
        in_specs=[HBM] * 3,
        out_specs=(VMEM, VMEM),
        scratch_shapes=[
            pltpu.SMEM(in_pattern.shape, in_pattern.dtype),
            pltpu.SMEM(out_pattern.shape, out_pattern.dtype),
            pltpu.VMEM(weights.shape, weights.dtype),
            pltpu.SemaphoreType.DMA((3,)),
        ],
        compiler_params=PARAMS,
        name="pack",
    )(in_hbm(in_pattern), in_hbm(out_pattern), in_hbm(weights))

    arrays, right_at = [packet], {0: (0, 0)}

    def keep(array, masks):
        arrays.append(array)
        right_at.update({m: (len(arrays) - 1, at) for at, m in enumerate(masks)})

    riding = gc_size == 8
    if riding:
        sums = pl.pallas_call(
            add_kernel,
            out_shape=jax.ShapeDtypeStruct(sums.shape, sums.dtype),
            in_specs=[VMEM] * 2,
            out_specs=VMEM,
            compiler_params=PARAMS,
            cost_estimate=LONG,
            name="add",
        )(sums, swap(sums, "gc", 5))
    else:
        sums = lax.psum(sums, "gc")
    for bit in reversed(bits_of(gc_size)):
        keep(swap(packet, "gc", bit), [bit])
    sums = jnp.concatenate([sums] + [swap(sums, "gr", m) for m in range(1, gr_size)], axis=0)

    hops = {}
    for mask in range(gc_size):
        if mask not in right_at and min(mask.bit_count(), max(2, gc_size.bit_length() - 2)) == 2:
            parent, hop = way_to(mask, "gc")
            hops.setdefault(hop, []).append((mask, parent))
    routes = [([right_at[parent][0] for _, parent in hop], riding) for hop in hops.values()]
    routes.append(([0, right_at[1][0]], False))
    extra = 2 * gr_size * blk_cols
    sent = pl.pallas_call(
        functools.partial(relay_kernel, routes, riding),
        out_shape=[
            jax.ShapeDtypeStruct((len(route) * rows + extra * rider, size), packet.dtype)
            for route, rider in routes
        ],
        in_specs=[VMEM] * (1 + len(arrays)),
        out_specs=[VMEM] * len(routes),
        compiler_params=PARAMS,
        name="relay",
    )(sums, *arrays)
    cores = [[i, i + 1] for i in range(0, gr_size, 2)]
    pairs = {0: sent[-1]}
    for bit in bits_of(gr_size)[:-1]:
        pairs.update({m | bit: swap(pair, "gr", bit) for m, pair in list(pairs.items())})
    lefts = [
        lax.all_gather(pair, "gr", axis_index_groups=cores, tiled=True) for pair in pairs.values()
    ]
    right, left = pl.pallas_call(
        functools.partial(spread_kernel, blk_rows, blk_cols, dict(right_at)),
        out_shape=(
            jax.ShapeDtypeStruct((order_size, local_cols), weights.dtype),
            jax.ShapeDtypeStruct((2 * local_rows, order_size), weights.dtype),
        ),
        in_specs=[VMEM] * len(arrays),
        out_specs=(VMEM, VMEM),
        compiler_params=PARAMS,
        name="spread",
    )(*arrays)
    early, riders = set(right_at), []
    for (hop, masks), buffer in zip(hops.items(), sent):
        keep(swap(buffer, "gc", hop), [m for m, _ in masks])
        if riding:
            riders.append((len(arrays) - 1, len(masks)))
    for mask in sorted(set(range(gc_size)) - set(right_at), key=lambda m: m.bit_count()):
        parent, hop = way_to(mask, "gc")
        n, at = right_at[parent]
        keep(swap(arrays[n][at * rows : (at + 1) * rows], "gc", hop), [mask])
    late_at = {m: at for m, at in right_at.items() if m not in early}
    inflated, sums, *_ = pl.pallas_call(
        functools.partial(expand_kernel, late_at, riders, list(pairs), blk_cols),
        out_shape=(jax.ShapeDtypeStruct(weights.shape, jnp.float32), sums_shape, right, left),
        in_specs=[VMEM] * (3 + len(lefts) + len(arrays)),
        out_specs=[VMEM] * 4,
        input_output_aliases={1 + len(lefts) + len(arrays): 2, 2 + len(lefts) + len(arrays): 3},
        compiler_params=PARAMS,
        name="expand",
    )(sums, *lefts, *arrays, right, left)
    totals = [sums] + [swap(sums, "gc", mask) for mask in range(2, gc_size, 2)]
    return pl.pallas_call(
        functools.partial(scale_kernel, float(order_size)),
        out_shape=jax.ShapeDtypeStruct(weights.shape, weights.dtype),
        in_specs=[VMEM] * (1 + len(totals)),
        out_specs=HBM,
        scratch_shapes=[
            pltpu.VMEM(weights.shape, weights.dtype),
            pltpu.SemaphoreType.DMA((CHUNKS,)),
        ],
        compiler_params=PARAMS,
        name="scale",
    )(inflated, *totals)


def solution(mesh):
    in_specs = (P("gc", "gr"), P("gc", "gr"), P("gc", "gr"))
    out_specs = P("gc", "gr")
    return jax.shard_map(shards, mesh=mesh, in_specs=in_specs, out_specs=out_specs, check_vma=False)
```

```python
import functools

import jax
import jax.numpy as jnp
from jax import lax
from jax.experimental import pallas as pl
from jax.experimental.pallas import tpu as pltpu
from jax.sharding import PartitionSpec as P

SLOTS = 4
META = 16
VMEM = pl.BlockSpec(memory_space=pltpu.VMEM)
HBM = pl.BlockSpec(memory_space=pltpu.HBM)
PARAMS = pltpu.CompilerParams(vmem_limit_bytes=16 << 20)
LONG = pl.CostEstimate(flops=10**10, bytes_accessed=0, transcendentals=0)


def in_hbm(x):
    return pltpu.with_memory_space_constraint(x, pltpu.HBM)


def bits_of(size):
    return [1 << b for b in reversed(range(size.bit_length() - 1))]


def swap(x, axis, mask):
    return lax.ppermute(x, axis, [(i, i ^ mask) for i in range(lax.axis_size(axis))])


def way_to(mask, axis):
    full = lax.axis_size(axis) - 1
    if mask == full and mask.bit_count() > 2:
        return 1, mask ^ 1
    bits = [bit for bit in bits_of(full + 1) if mask & bit]
    last = bits[min(1, len(bits) - 1)]
    return mask ^ last, last


def places_in(packet, size):
    meta = packet[pl.ds(SLOTS * size, META), :].astype(jnp.float32)
    meta = meta.astype(jnp.int32)
    return [meta[s, 0] for s in range(SLOTS)]


def pack_kernel(flags_hbm, kept_hbm, weights_hbm, packet_ref, sums_ref, flags_ref, kept_ref, weights_ref, sems):
    copies = [
        pltpu.make_async_copy(flags_hbm, flags_ref, sems.at[0]),
        pltpu.make_async_copy(kept_hbm, kept_ref, sems.at[1]),
        pltpu.make_async_copy(weights_hbm, weights_ref, sems.at[2]),
    ]
    for copy in copies:
        copy.start()
    for copy in copies:
        copy.wait()
    blk_rows, blk_cols = flags_ref.shape
    size = weights_ref.shape[0] // blk_rows
    blocks = blk_rows * blk_cols
    flags = [flags_ref[b // blk_cols, b % blk_cols] for b in range(blocks)]
    count = sum(flags)
    ones, zeros, slots = 0, 0, []
    for b in range(blocks):
        slots.append(jnp.where(flags[b] == 1, ones, count + zeros))
        ones, zeros = ones + flags[b], zeros + (1 - flags[b])
    sums_ref[...] = jnp.zeros_like(sums_ref)
    row_ids = lax.broadcasted_iota(jnp.int32, (META, size), 0)
    meta = jnp.zeros((META, size), jnp.float32)
    for s in range(SLOTS):
        place = sum(jnp.where(slots[b] == s, b, 0) for b in range(blocks))
        row = pl.multiple_of(place // blk_cols * size, size)
        col = pl.multiple_of(place % blk_cols * size, size)
        block = weights_ref[pl.ds(row, size), pl.ds(col, size)]
        block = jnp.where(s < count, block, jnp.zeros_like(block))
        packet_ref[pl.ds(s * size, size), :] = block
        sums_ref[:, pl.ds(col, size)] += jnp.sum(block.astype(jnp.float32), axis=0, keepdims=True)
        meta = jnp.where(row_ids == s, place.astype(jnp.float32), meta)
    for b in range(blocks):
        kept = kept_ref[b // blk_cols, b % blk_cols].astype(jnp.float32)
        meta = jnp.where(row_ids == SLOTS + b, kept, meta)
    packet_ref[pl.ds(SLOTS * size, META), :] = meta.astype(packet_ref.dtype)


def rows_of(sums_ref):
    size = 128
    parts = [
        sums_ref[r : r + 1, at : at + size]
        for r in range(sums_ref.shape[0])
        for at in range(0, sums_ref.shape[1], size)
    ]
    return jnp.concatenate(parts, axis=0)


def split(x):
    high = x.astype(jnp.bfloat16)
    return high, (x - high.astype(jnp.float32)).astype(jnp.bfloat16)


def add_kernel(one_ref, other_ref, out_ref):
    out_ref[...] = one_ref[...] + other_ref[...]


def relay_kernel(routes, riding, sums_ref, *refs):
    packet_refs, sent_refs = refs[: -len(routes)], refs[-len(routes) :]
    rows = packet_refs[0].shape[0]
    if riding:
        high, low = split(rows_of(sums_ref))
    for sent_ref, (route, rider) in zip(sent_refs, routes):
        for at, source in enumerate(route):
            sent_ref[pl.ds(at * rows, rows), :] = packet_refs[source][...]
        if rider:
            first = len(route) * rows
            sent_ref[pl.ds(first, high.shape[0]), :] = high
            sent_ref[pl.ds(first + high.shape[0], high.shape[0]), :] = low


def spread(blk_rows, blk_cols, size, packets, right):
    my_row = lax.axis_index("gc")
    for m, packet in packets.items():
        base = (my_row ^ m) * blk_rows
        for s, place in enumerate(places_in(packet, size)):
            row = pl.multiple_of((base + place // blk_cols) * size, size)
            col = pl.multiple_of(place % blk_cols * size, size)
            right[pl.ds(row, size), pl.ds(col, size)] = packet[pl.ds(s * size, size), :]


def packets_in(refs, table, rows):
    return {m: refs[n].at[pl.ds(at * rows, rows), :] for m, (n, at) in table.items()}


def spread_kernel(blk_rows, blk_cols, right_at, *refs):
    *refs, right, left = refs
    rows, size = refs[0].shape
    right[...] = jnp.zeros_like(right)
    left[...] = jnp.zeros_like(left)
    spread(blk_rows, blk_cols, size, packets_in(refs, right_at, rows), right)


def expand_kernel(right_at, riders, evens, blk_cols, sums_ref, *refs):
    *pairs, _, _, inflated_ref, total_ref, right, left = refs[: len(evens)] + refs[-6:]
    refs = refs[len(evens) : -6]
    rows, size = refs[0].shape
    blk_rows = inflated_ref.shape[0] // size
    spread(blk_rows, blk_cols, size, packets_in(refs, right_at, rows), right)
    sums = rows_of(sums_ref)
    for n, at in riders:
        high = refs[n][pl.ds(at * rows, sums.shape[0]), :].astype(jnp.float32)
        low = refs[n][pl.ds(at * rows + sums.shape[0], sums.shape[0]), :].astype(jnp.float32)
        sums = sums + (high + low)
    inverse = 1.0 / sums
    my_col = lax.axis_index("gr")
    for n in range(2 * len(evens)):
        gr = my_col // 2 * 2 + n % 2 ^ evens[n // 2]
        scales = []
        for j in range(blk_cols):
            scale = inverse[j : j + 1]
            for m in range(1, 2 * len(evens)):
                there = inverse[m * blk_cols + j : m * blk_cols + j + 1]
                scale = jnp.where(my_col ^ m == gr, there, scale)
            scales.append(scale)
        for part in range(2):
            packet = pairs[n // 2].at[pl.ds((n % 2 * 2 + part) * rows, rows), :]
            for s, place in enumerate(places_in(packet, size)):
                row = pl.multiple_of((part * blk_rows + place // blk_cols) * size, size)
                col = place % blk_cols
                scale = scales[0]
                for j in range(1, blk_cols):
                    scale = jnp.where(col == j, scales[j], scale)
                block = packet[pl.ds(s * size, size), :].astype(jnp.float32) * scale
                at = pl.multiple_of((gr * blk_cols + col) * size, size)
                left[pl.ds(row, size), pl.ds(at, size)] = block.astype(left.dtype)
    product = jnp.dot(left[...], right[...], preferred_element_type=jnp.float32)
    first = SLOTS * size
    flags = [ref[pl.ds(first, META), :].astype(jnp.float32) for ref in (refs[0], refs[1])]
    for j in range(blk_cols):
        at = slice(j * size, (j + 1) * size)
        own = inverse[j : j + 1]
        total = jnp.zeros((1, size), jnp.float32)
        for i in range(2 * blk_rows):
            part, flag = i // blk_rows, SLOTS + i % blk_rows * blk_cols + j
            kept = product[i * size : (i + 1) * size, at] * own
            kept = kept * flags[part][flag : flag + 1]
            squared = kept * kept
            if part == 0:
                inflated_ref[i * size : (i + 1) * size, at] = squared
            total = total + jnp.sum(squared, axis=0, keepdims=True)
        total_ref[:, at] = total


def shards(weights, in_pattern, out_pattern):
    blk_rows, blk_cols = in_pattern.shape
    local_rows, local_cols = weights.shape
    size = local_rows // blk_rows
    gr_size, gc_size = lax.axis_size("gr"), lax.axis_size("gc")
    order_size = local_rows * gc_size
    sums_shape = jax.ShapeDtypeStruct((1, local_cols), jnp.float32)
    rows = SLOTS * size + META
    packet, sums = pl.pallas_call(
        pack_kernel,
        out_shape=(jax.ShapeDtypeStruct((rows, size), weights.dtype), sums_shape),
        in_specs=[HBM] * 3,
        out_specs=(VMEM, VMEM),
        scratch_shapes=[
            pltpu.SMEM(in_pattern.shape, in_pattern.dtype),
            pltpu.SMEM(out_pattern.shape, out_pattern.dtype),
            pltpu.VMEM(weights.shape, weights.dtype),
            pltpu.SemaphoreType.DMA((3,)),
        ],
        compiler_params=PARAMS,
        name="pack",
    )(in_hbm(in_pattern), in_hbm(out_pattern), in_hbm(weights))

    arrays, right_at = [packet], {0: (0, 0)}

    def keep(array, masks):
        arrays.append(array)
        right_at.update({m: (len(arrays) - 1, at) for at, m in enumerate(masks)})

    riding = gc_size == 8
    if riding:
        sums = pl.pallas_call(
            add_kernel,
            out_shape=jax.ShapeDtypeStruct(sums.shape, sums.dtype),
            in_specs=[VMEM] * 2,
            out_specs=VMEM,
            compiler_params=PARAMS,
            cost_estimate=LONG,
            name="add",
        )(sums, swap(sums, "gc", 5))
    else:
        sums = lax.psum(sums, "gc")
    for bit in reversed(bits_of(gc_size)):
        keep(swap(packet, "gc", bit), [bit])
    sums = jnp.concatenate([sums] + [swap(sums, "gr", m) for m in range(1, gr_size)], axis=0)

    hops = {}
    for mask in range(gc_size):
        if mask not in right_at and min(mask.bit_count(), max(2, gc_size.bit_length() - 2)) == 2:
            parent, hop = way_to(mask, "gc")
            hops.setdefault(hop, []).append((mask, parent))
    routes = [([right_at[parent][0] for _, parent in hop], riding) for hop in hops.values()]
    routes.append(([0, right_at[1][0]], False))
    extra = 2 * gr_size * blk_cols
    sent = pl.pallas_call(
        functools.partial(relay_kernel, routes, riding),
        out_shape=[
            jax.ShapeDtypeStruct((len(route) * rows + extra * rider, size), packet.dtype)
            for route, rider in routes
        ],
        in_specs=[VMEM] * (1 + len(arrays)),
        out_specs=[VMEM] * len(routes),
        compiler_params=PARAMS,
        name="relay",
    )(sums, *arrays)
    first = list(arrays)
    first_at = dict(right_at)
    early, riders = set(right_at), []
    for (hop, masks), buffer in zip(hops.items(), sent):
        keep(swap(buffer, "gc", hop), [m for m, _ in masks])
        if riding:
            riders.append((len(arrays) - 1, len(masks)))
    cores = [[i, i + 1] for i in range(0, gr_size, 2)]
    pairs = {0: sent[-1]}
    for bit in bits_of(gr_size)[:-1]:
        pairs.update({m | bit: swap(pair, "gr", bit) for m, pair in list(pairs.items())})
    lefts = [
        lax.all_gather(pair, "gr", axis_index_groups=cores, tiled=True) for pair in pairs.values()
    ]
    right, left = pl.pallas_call(
        functools.partial(spread_kernel, blk_rows, blk_cols, first_at),
        out_shape=(
            jax.ShapeDtypeStruct((order_size, local_cols), weights.dtype),
            jax.ShapeDtypeStruct((2 * local_rows, order_size), weights.dtype),
        ),
        in_specs=[VMEM] * len(first),
        out_specs=(VMEM, VMEM),
        compiler_params=PARAMS,
        name="spread",
    )(*first)
    for mask in sorted(set(range(gc_size)) - set(right_at), key=lambda m: m.bit_count()):
        parent, hop = way_to(mask, "gc")
        n, at = right_at[parent]
        keep(swap(arrays[n][at * rows : (at + 1) * rows], "gc", hop), [mask])
    late_at = {m: at for m, at in right_at.items() if m not in early}
    inflated, sums, *_ = pl.pallas_call(
        functools.partial(expand_kernel, late_at, riders, list(pairs), blk_cols),
        out_shape=(jax.ShapeDtypeStruct(weights.shape, jnp.float32), sums_shape, right, left),
        in_specs=[VMEM] * (3 + len(lefts) + len(arrays)),
        out_specs=[VMEM] * 4,
        input_output_aliases={1 + len(lefts) + len(arrays): 2, 2 + len(lefts) + len(arrays): 3},
        compiler_params=PARAMS,
        name="expand",
    )(sums, *lefts, *arrays, right, left)
    output_total = sums
    for mask in range(2, gc_size, 2):
        output_total = output_total + swap(sums, "gc", mask)
    return (inflated / output_total * float(order_size)).astype(jnp.bfloat16)


def solution(mesh):
    in_specs = (P("gc", "gr"), P("gc", "gr"), P("gc", "gr"))
    out_specs = P("gc", "gr")
    return jax.shard_map(shards, mesh=mesh, in_specs=in_specs, out_specs=out_specs, check_vma=False)
```
